512 devices in a mesh: freq: 16 (over y, z_hi, core), sx: 8 (over z_lo), sy: 4 (over x).
Axes of the slice: x: 4, y: 4, z: 16 (z_hi: 2, z_lo: 8; z = z_hi * 8 + z_lo), core: 2. Of those that a mesh axis runs over, the one named last changes fastest.
Arguments:
- source: float32 [2, 32, 512, 1024], P(None, 'freq', 'sx', 'sy'), may hold values from -6 to 6
- receiver: float32 [2, 32, 512, 1024], P(None, 'freq', 'sx', 'sy'), may hold values from -6 to 6
- table_index: int32 [2, 32, 512, 1024], P(None, 'freq', 'sx', 'sy'), may hold values from 0 to 31
- coef_table: float32 [2, 32, 13], replicated, may hold values from -1.2 to 1.2
Outputs:
- source_out: float32 [2, 32, 512, 1024], P(None, 'freq', 'sx', 'sy')
- receiver_out: float32 [2, 32, 512, 1024], P(None, 'freq', 'sx', 'sy')
- image: float32 [2, 512, 1024], P(None, 'sx', 'sy')
The draws below stay inside these ranges and needn't reach their ends.
All inputs are finite; a program needn't handle non-finite values.
Results may differ from the reference program's by a relative error of at most 0.0003.
Values sent between devices are 32-bit elements; how exact they have to be, the bound alone decides.
No kernel may reach another device: no remote copies, remote signals or barrier semaphores. Data moves between devices by JAX's collectives and lax.ppermute only.
A program may use at most 64 MiB of HBM per device.

```python
import jax
import jax.numpy as jnp

NCOEF = 13
NTAB = 32
DEPTHS = 2
NF = 32
NX = 512
NY = 1024


def place_ends(values, own_key, low, high):
    spot = [jax.random.randint(jax.random.fold_in(own_key, axis), (), 0, length) for axis, length in enumerate(values.shape)]
    main_axis = values.shape.index(max(values.shape))
    next_to = spot[:main_axis] + [(spot[main_axis] + 1) % values.shape[main_axis]] + spot[main_axis + 1:]
    return values.at[tuple(spot)].set(low).at[tuple(next_to)].set(high)


def shard_levels(stream_key, extent, cuts, low, top_value):
    loudness = 1.0
    for axis_at, blocks in cuts:
        heights = jax.random.uniform(jax.random.fold_in(jax.random.fold_in(stream_key, 6), axis_at), (blocks,), jnp.float32, low / len(cuts), top_value / len(cuts))
        loudness = loudness * jnp.repeat(jnp.exp(heights), extent[axis_at] // blocks).reshape((-1,) + (1,) * (len(extent) - 1 - axis_at))
    return loudness


def scatter_about(key, extent, spread, reach, pieces=(), held_as=jnp.bfloat16):
    result = jax.random.normal(key, extent, jnp.float32) * spread
    if len(pieces) > 0:
        result = shard_levels(key, extent, pieces, -0.22, 0.18) * result
    return jnp.clip(result, min=-reach, max=reach).astype(held_as)


def setup_inputs(seed: int = 0) -> dict:
    key_of = jax.random.split(jax.random.key(seed), 5)
    return {
        "source": scatter_about(key_of[0], (2, NF, NX, NY), 1.0, 6.0, ((1, 16), (2, 8), (3, 4)), jnp.float32),
        "receiver": scatter_about(key_of[1], (2, NF, NX, NY), 1.0, 6.0, ((1, 16), (2, 8), (3, 4)), jnp.float32),
        "table_index": place_ends(jax.random.randint(key_of[2], (DEPTHS, NF, NX, NY), 0, NTAB), jax.random.fold_in(key_of[2], 1), 0, NTAB - 1).astype(jnp.int32),
        "coef_table": scatter_about(key_of[3], (2, NTAB, NCOEF), 0.3, 1.2, (), jnp.float32),
    }


def stencil(padded):
    centre = padded[..., 1:-1, 1:-1]
    edges = padded[..., 2:, 1:-1] + padded[..., :-2, 1:-1] + padded[..., 1:-1, 2:] + padded[..., 1:-1, :-2]
    corners = padded[..., 2:, 2:] + padded[..., 2:, :-2] + padded[..., :-2, 2:] + padded[..., :-2, :-2]
    return -0.5 * centre + 0.25 * edges + 0.125 * corners


def operate(field):
    pads = [(0, 0)] * (field.ndim - 2) + [(1, 1), (1, 1)]
    return stencil(jnp.pad(field, pads))


def combine(coef_re, coef_im, term, signs):
    real_part = coef_re * term[:, 0] - signs * coef_im * term[:, 1]
    imag_part = signs * coef_im * term[:, 0] + coef_re * term[:, 1]
    return jnp.stack([real_part, imag_part], axis=1)


def reference(source, receiver, table_index, coef_table):
    waves = jnp.stack([source, receiver])
    signs = jnp.array([1.0, -1.0], jnp.float32).reshape(2, 1, 1, 1)
    images = []
    for depth in range(DEPTHS):
        index_now = table_index[depth]

        def coefs(order):
            return jnp.take(coef_table[0, :, order], index_now), jnp.take(coef_table[1, :, order], index_now)

        previous = waves
        current = operate(waves)
        re0, im0 = coefs(0)
        re1, im1 = coefs(1)
        total = combine(re0, im0, previous, signs) + combine(re1, im1, current, signs)
        for order in range(2, NCOEF):
            following = 2.0 * operate(current) - previous
            rek, imk = coefs(order)
            total = total + combine(rek, imk, following, signs)
            previous, current = current, following
        waves = total
        images.append(jnp.sum(waves[0] * waves[1], axis=(0, 1)))
    return waves[0], waves[1], jnp.stack(images)
```

```python
import jax
import jax.numpy as jnp
from jax import lax
from jax.experimental import pallas as pl
from jax.experimental.pallas import tpu as pltpu
from jax.sharding import PartitionSpec as P

ROWS, COLS = 64, 256
HALO = 24
SIDE = 32
STEPS = 5
FIRST = ROWS + 2 * HALO
SECOND = ROWS + HALO
INDEX_HALO = 16
SEND = 4 * STEPS * HALO + STEPS * INDEX_HALO
WIDE = STEPS * 128
VMEM = 48 * 1024 * 1024


def spread_matrix():
    k = lax.broadcasted_iota(jnp.int32, (WIDE, WIDE), 0)
    n = lax.broadcasted_iota(jnp.int32, (WIDE, WIDE), 1)
    step, lane = n // 128, n % 128
    wave, column = lane // 64, (lane % 64) * STEPS + step
    own = k < 2 * COLS
    edge = k - 2 * COLS
    from_wave = jnp.where(own, k // COLS, (edge // SIDE) % 2)
    from_column = jnp.where(own, SIDE + k % COLS, jnp.where(edge < 2 * SIDE, 0, SIDE + COLS) + edge % SIDE)
    return ((wave == from_wave) & (column == from_column)).astype(jnp.bfloat16)


def dot(left, right, contract):
    return lax.dot_general(left, right, (contract, ((), ())), preferred_element_type=jnp.float32)


def exact_dot(left, right, contract):
    high = left.astype(jnp.bfloat16)
    rest = left - high.astype(jnp.float32)
    middle = rest.astype(jnp.bfloat16)
    low = (rest - middle.astype(jnp.float32)).astype(jnp.bfloat16)
    return dot(high, right, contract) + dot(middle, right, contract) + dot(low, right, contract)


def edges_kernel(source, receiver, index, left, right):
    lane = lax.broadcasted_iota(jnp.int32, (ROWS, 128), 1)

    def join(parts, start):
        total = jnp.zeros((ROWS, 128), jnp.float32)
        for place, part in enumerate(parts):
            shift = (place * SIDE - start) % 128
            moved = part if shift == 0 else pltpu.roll(part, shift, 1)
            total = jnp.where((lane >= place * SIDE) & (lane < (place + 1) * SIDE), moved, total)
        return total

    for out, tile, start in ((left, 0, 0), (right, 1, 128 - SIDE)):
        cut = slice(tile * 128, (tile + 1) * 128)
        for place, waves in enumerate((source, receiver)):
            out[place] = join([waves[part, wave, :, cut] for part in range(2) for wave in range(2)], start)
        out[2] = join([index[wave, :, cut].astype(jnp.float32) for wave in range(2)], start)


def spread_kernel(source, receiver, index0, index1, low, high, spread, fields, indices0, indices1, top, bottom, joined, joined_index):
    lane = lax.broadcasted_iota(jnp.int32, (ROWS, 128), 1)

    def halos(place, part):
        from_low, from_high = low[place], high[place]
        if part == 0:
            return jnp.where(lane < 64, from_low, pltpu.roll(from_high, 64, 1))
        return jnp.where(lane < 64, pltpu.roll(from_low, 64, 1), from_high)

    for plane in range(4):
        waves, part = (source, receiver)[plane // 2], plane % 2
        rows = slice(plane * ROWS, (plane + 1) * ROWS)
        for wave in range(2):
            joined[rows, wave * COLS : (wave + 1) * COLS] = waves[part, wave]
        joined[rows, 2 * COLS :] = halos(plane // 2, part)
    for depth, index in enumerate((index0, index1)):
        rows = slice(depth * ROWS, (depth + 1) * ROWS)
        for wave in range(2):
            joined_index[rows, wave * COLS : (wave + 1) * COLS] = index[wave].astype(jnp.float32)
        joined_index[rows, 2 * COLS :] = halos(2, 0) if depth == 0 else jnp.zeros((ROWS, 128), jnp.float32)

    matrix = spread[...]
    for plane in range(4):
        values = exact_dot(joined[plane * ROWS : (plane + 1) * ROWS, :], matrix, ((1,), (0,)))
        for step in range(STEPS):
            piece = values[:, step * 128 : (step + 1) * 128]
            fields[plane, step] = piece
            at = (plane * STEPS + step) * HALO
            top[at : at + HALO, :] = piece[:HALO]
            bottom[at : at + HALO, :] = piece[ROWS - HALO :]
    values = dot(joined_index[...].astype(jnp.bfloat16), matrix, ((1,), (0,)))
    for step in range(STEPS):
        piece = values[:ROWS, step * 128 : (step + 1) * 128]
        indices0[step] = piece
        at = 4 * STEPS * HALO + step * INDEX_HALO
        top[at : at + INDEX_HALO, :] = piece[:INDEX_HALO]
        bottom[at : at + INDEX_HALO, :] = piece[ROWS - INDEX_HALO :]
        indices1[step] = values[ROWS:, step * 128 : (step + 1) * 128]


def march_kernel(
    flags, fields, indices0, indices1, above, below, table, spread, source_out, receiver_out, image,
    terms, masks, places, picture, result,
):
    orders = terms.shape[0]
    for plane in range(4):
        for step in range(STEPS):
            at = (plane * STEPS + step) * HALO
            terms[0, plane, step, :HALO, :] = above[at : at + HALO, :]
            terms[0, plane, step, HALO : HALO + ROWS, :] = fields[plane, step]
            terms[0, plane, step, HALO + ROWS :, :] = below[at : at + HALO, :]
    for step in range(STEPS):
        at = 4 * STEPS * HALO + step * INDEX_HALO
        places[0, step, HALO - INDEX_HALO : HALO, :] = above[at : at + INDEX_HALO, :].astype(jnp.int32)
        places[0, step, HALO : HALO + ROWS, :] = indices0[step].astype(jnp.int32)
        places[0, step, HALO + ROWS : HALO + ROWS + INDEX_HALO, :] = below[at : at + INDEX_HALO, :].astype(jnp.int32)
        places[1, step] = jnp.zeros((FIRST, 128), jnp.int32)
        places[1, step, HALO : HALO + ROWS, :] = indices1[step].astype(jnp.int32)

    lane = lax.broadcasted_iota(jnp.int32, (FIRST, 128), 1)
    row = lax.broadcasted_iota(jnp.int32, (FIRST, 128), 0)
    inside_row = jnp.where(row < HALO, flags[0], jnp.where(row >= HALO + ROWS, flags[1], 1.0))
    for step in range(STEPS):
        column = (lane % 64) * STEPS + step
        inside_column = jnp.where(column < SIDE, flags[2], jnp.where(column >= SIDE + COLS, flags[3], 1.0))
        masks[step] = 0.25 * inside_row * inside_column

    def depth_step(depth, base, count):
        def rows(r):
            return pl.ds(base + r, 8, stride=count)

        def advance(plane, now, first):
            def load(r):
                return [terms[now, plane, step, rows(r), :] for step in range(STEPS)]

            start = load(0)
            last = load(count - 1)
            wrapped = [pltpu.roll(v, 7, 0) for v in start]
            pair = [pltpu.roll(a + b, 1, 0) for a, b in zip(last, wrapped)]
            value = start
            for r in range(count):
                after = load(r + 1) if r + 1 < count else wrapped
                new_pair = [a + b for a, b in zip(value, after)]
                column = [a + b for a, b in zip(pair, new_pair)]
                right = [column[s] + column[s + 1] for s in range(STEPS - 1)]
                right.append(column[STEPS - 1] + pltpu.roll(column[0], 127, 1))
                both = [pltpu.roll(right[STEPS - 1], 1, 1) + right[0]]
                both += [right[s - 1] + right[s] for s in range(1, STEPS)]
                for step in range(STEPS):
                    moved = masks[step, rows(r), :] * both[step]
                    if first:
                        new = 0.5 * moved - value[step]
                    else:
                        new = (moved - (value[step] + value[step])) - terms[now - 1, plane, step, rows(r), :]
                    terms[now + 1, plane, step, rows(r), :] = new
                pair, value = new_pair, after

        def first_order(plane, carry):
            advance(plane, 0, True)
            return carry

        lax.fori_loop(0, 4, first_order, 0)

        def other_orders(count_down, carry):
            advance(lax.rem(count_down, 4), 1 + lax.div(count_down, 4), False)
            return carry

        lax.fori_loop(0, 4 * (orders - 2), other_orders, 0)

        def combine(r, carry):
            out_rows = pl.ds(HALO // 2 + r, 8, stride=SECOND // 8)
            for step in range(STEPS):
                place = places[depth, step, out_rows, :]
                total = [None] * 4
                for order in range(orders):
                    re = jnp.take_along_axis(jnp.broadcast_to(table[order, :][None], (8, 128)), place, axis=1)
                    im = jnp.take_along_axis(jnp.broadcast_to(table[orders + order, :][None], (8, 128)), place, axis=1)
                    for waves, sign in ((0, 1), (2, -1)):
                        real = terms[order, waves, step, out_rows, :]
                        imag = terms[order, waves + 1, step, out_rows, :]
                        if sign > 0:
                            new = (re * real - im * imag, re * imag + im * real)
                        else:
                            new = (re * real + im * imag, re * imag - im * real)
                        for part in range(2):
                            old = total[waves + part]
                            total[waves + part] = new[part] if old is None else old + new[part]
                for plane in range(4):
                    terms[0, plane, step, out_rows, :] = total[plane]
                picture[depth, step, out_rows, :] = total[0] * total[2] + total[1] * total[3]
            return carry

        lax.fori_loop(0, SECOND // 8, combine, 0)

    depth_step(0, 0, FIRST // 8)
    depth_step(1, HALO // 2, SECOND // 8)

    own = slice(HALO, HALO + ROWS)
    matrix = spread[: 2 * COLS, :]
    for plane in range(6):
        for step in range(STEPS):
            piece = terms[0, plane, step, own, :] if plane < 4 else picture[plane - 4, step, own, :]
            result[plane * ROWS : (plane + 1) * ROWS, step * 128 : (step + 1) * 128] = piece
    for plane in range(6):
        values = exact_dot(result[plane * ROWS : (plane + 1) * ROWS, :], matrix, ((1,), (1,)))
        if plane < 4:
            out = (source_out, receiver_out)[plane // 2]
            for wave in range(2):
                out[plane % 2, wave] = values[:, wave * COLS : (wave + 1) * COLS]
        else:
            total = values[:, :COLS] + values[:, COLS:]
            for part in range(8):
                image[part, plane - 4] = total[part * 8 : (part + 1) * 8]


def full(count):
    return [pl.BlockSpec(memory_space=pltpu.VMEM)] * count


def shape(*dims, dtype=jnp.float32):
    return jax.ShapeDtypeStruct(dims, dtype)


def params():
    return pltpu.CompilerParams(vmem_limit_bytes=VMEM)


def shift(block, axis, forward):
    count = lax.axis_size(axis)
    pairs = [(i, i + 1) for i in range(count - 1)]
    return lax.ppermute(block, axis, pairs if forward else [(b, a) for a, b in pairs])


def extrapolate(source, receiver, table_index, coef_table):
    orders = coef_table.shape[2]
    spread = spread_matrix()
    left, right = pl.pallas_call(
        edges_kernel,
        out_shape=(shape(3, ROWS, 128), shape(3, ROWS, 128)),
        in_specs=full(3),
        out_specs=tuple(full(2)),
        compiler_params=params(),
        name="edges",
    )(source, receiver, table_index[0])
    low = shift(right, "sy", True)
    high = shift(left, "sy", False)
    fields, indices0, indices1, top, bottom = pl.pallas_call(
        spread_kernel,
        out_shape=(
            shape(4, STEPS, ROWS, 128),
            shape(STEPS, ROWS, 128),
            shape(STEPS, ROWS, 128),
            shape(SEND, 128),
            shape(SEND, 128),
        ),
        in_specs=full(7),
        out_specs=tuple(full(5)),
        scratch_shapes=[pltpu.VMEM((4 * ROWS, WIDE), jnp.float32), pltpu.VMEM((2 * ROWS, WIDE), jnp.float32)],
        compiler_params=params(),
        name="spread",
    )(source, receiver, table_index[0], table_index[1], low, high, spread)
    above = shift(bottom, "sx", True)
    below = shift(top, "sx", False)
    at_x, at_y = lax.axis_index("sx"), lax.axis_index("sy")
    flags = jnp.stack(
        [at_x > 0, at_x < lax.axis_size("sx") - 1, at_y > 0, at_y < lax.axis_size("sy") - 1]
    ).astype(jnp.float32)
    table = jnp.pad(jnp.swapaxes(coef_table, 1, 2).reshape(2 * orders, -1), ((0, 0), (0, 128 - coef_table.shape[1])))
    return pl.pallas_call(
        march_kernel,
        out_shape=(shape(2, 2, ROWS, COLS), shape(2, 2, ROWS, COLS), shape(8, 2, 8, COLS)),
        in_specs=[pl.BlockSpec(memory_space=pltpu.SMEM)] + full(7),
        out_specs=tuple(full(3)),
        scratch_shapes=[
            pltpu.VMEM((orders, 4, STEPS, FIRST, 128), jnp.float32),
            pltpu.VMEM((STEPS, FIRST, 128), jnp.float32),
            pltpu.VMEM((2, STEPS, FIRST, 128), jnp.int32),
            pltpu.VMEM((2, STEPS, FIRST, 128), jnp.float32),
            pltpu.VMEM((6 * ROWS, WIDE), jnp.float32),
        ],
        compiler_params=params(),
        name="march",
    )(flags, fields, indices0, indices1, above, below, table, spread)


def add_over_freq(pieces):
    groups = [[y * 4 + z * 2 + core for y in range(4) for core in range(2)] for z in range(2)]
    mine = jnp.sum(lax.all_to_all(pieces, "freq", 0, 0, axis_index_groups=groups), axis=0)
    mine = mine + lax.ppermute(mine, "freq", [(i, i ^ 2) for i in range(16)])
    blocks = lax.all_to_all(jnp.broadcast_to(mine[None], pieces.shape), "freq", 0, 0, axis_index_groups=groups)
    return jnp.swapaxes(blocks, 0, 1).reshape(2, ROWS, COLS)


def local(source, receiver, table_index, coef_table):
    source_out, receiver_out, pieces = extrapolate(source, receiver, table_index, coef_table)
    return source_out, receiver_out, add_over_freq(pieces)


def solution(mesh):
    placed = P(None, "freq", "sx", "sy")
    return jax.shard_map(
        local,
        mesh=mesh,
        in_specs=(placed, placed, placed, P()),
        out_specs=(placed, placed, P(None, "sx", "sy")),
        check_vma=False,
    )
```

```python
import jax
import jax.numpy as jnp
from jax import lax
from jax.experimental import pallas as pl
from jax.experimental.pallas import tpu as pltpu
from jax.sharding import PartitionSpec as P

ROWS, COLS = 64, 256
HALO = 24
HALF = HALO // 2
SIDE = 32
STEPS = 5
INDEX_HALO = 16
FIELD_ROWS = 4 * STEPS * HALO
SEND = FIELD_ROWS + STEPS * INDEX_HALO
WIDE = STEPS * 128
STRIP = 16
OFFSET = 32
TALL = 128
INNER = slice(HALO, ROWS - HALO)


def spread_matrix():
    k = lax.broadcasted_iota(jnp.int32, (WIDE, WIDE), 0)
    n = lax.broadcasted_iota(jnp.int32, (WIDE, WIDE), 1)
    step, lane = n // 128, n % 128
    wave, column = lane // 64, (lane % 64) * STEPS + step
    own = k < 2 * COLS
    edge = k - 2 * COLS
    from_wave = jnp.where(own, k // COLS, (edge // SIDE) % 2)
    from_column = jnp.where(own, SIDE + k % COLS, jnp.where(edge < 2 * SIDE, 0, SIDE + COLS) + edge % SIDE)
    return ((wave == from_wave) & (column == from_column)).astype(jnp.bfloat16)


def dot(left, right, contract):
    return lax.dot_general(left, right, (contract, ((), ())), preferred_element_type=jnp.float32)


def exact_dot(left, right, contract):
    high = left.astype(jnp.bfloat16)
    rest = left - high.astype(jnp.float32)
    middle = rest.astype(jnp.bfloat16)
    low = (rest - middle.astype(jnp.float32)).astype(jnp.bfloat16)
    return dot(high, right, contract) + dot(middle, right, contract) + dot(low, right, contract)


def edges_kernel(source, receiver, index, left, right, waves, places, sems):
    copies = [
        pltpu.make_async_copy(source, waves.at[0], sems.at[0]),
        pltpu.make_async_copy(receiver, waves.at[1], sems.at[1]),
        pltpu.make_async_copy(index.at[0], places, sems.at[2]),
    ]
    for copy in copies:
        copy.start()
    lane = lax.broadcasted_iota(jnp.int32, (ROWS, 128), 1)

    def join(parts, start):
        total = jnp.zeros((ROWS, 128), jnp.float32)
        for place, part in enumerate(parts):
            shift = (place * SIDE - start) % 128
            moved = part if shift == 0 else pltpu.roll(part, shift, 1)
            total = jnp.where((lane >= place * SIDE) & (lane < (place + 1) * SIDE), moved, total)
        return total

    ends = ((right, 1, 128 - SIDE), (left, 0, 0))
    for kind in range(3):
        copies[kind].wait()
        for out, tile, start in ends:
            cut = slice(tile * 128, (tile + 1) * 128)
            if kind < 2:
                out[kind] = join([waves[kind, part, wave, :, cut] for part in range(2) for wave in range(2)], start)
            else:
                out[2] = join([places[wave, :, cut].astype(jnp.float32) for wave in range(2)], start)


def own_kernel(source, receiver, index, spread, fields, indices, joined):
    matrix = spread[: 2 * COLS, :]
    for plane in range(6):
        for wave in range(2):
            cut = slice(wave * COLS, (wave + 1) * COLS)
            if plane < 4:
                joined[:, cut] = (source, receiver)[plane // 2][plane % 2, wave]
            else:
                joined[:, cut] = index[plane - 4, wave].astype(jnp.float32)
        if plane < 4:
            values = exact_dot(joined[...], matrix, ((1,), (0,)))
        else:
            values = dot(joined[...].astype(jnp.bfloat16), matrix, ((1,), (0,)))
        for step in range(STEPS):
            piece = values[:, step * 128 : (step + 1) * 128]
            if plane < 4:
                fields[plane, step] = piece
            else:
                indices[plane - 4, step] = piece


def merge_kernel(own, indices, low, high, spread, fields, indices0, top, bottom, joined):
    lane = lax.broadcasted_iota(jnp.int32, (ROWS, 128), 1)
    matrix = spread[2 * COLS :, :]
    for plane in range(5):
        from_low, from_high = low[plane // 2], high[plane // 2]
        if plane % 2 == 0:
            from_high = pltpu.roll(from_high, 64, 1)
        else:
            from_low = pltpu.roll(from_low, 64, 1)
        joined[plane * ROWS : (plane + 1) * ROWS, :] = jnp.where(lane < 64, from_low, from_high)
    values = exact_dot(joined[...], matrix, ((1,), (0,)))
    for plane in range(5):
        for step in range(STEPS):
            piece = values[plane * ROWS : (plane + 1) * ROWS, step * 128 : (step + 1) * 128]
            if plane < 4:
                piece = piece + own[plane, step]
                fields[plane, step] = piece
                rows, at = HALO, (plane * STEPS + step) * HALO
            else:
                piece = piece + indices[0, step]
                indices0[step] = piece
                rows, at = INDEX_HALO, FIELD_ROWS + step * INDEX_HALO
            top[at : at + rows, :] = piece[:rows]
            bottom[at : at + rows, :] = piece[ROWS - rows :]


def advance(terms, past, plane, origin, ahead, count, mask, first):
    now = 0 if first else past + 1

    def rows(first_row):
        return pl.ds(first_row, 8, stride=count)

    def load(r):
        return [terms[now, plane, step, rows(origin + ahead + r), :] for step in range(STEPS)]

    values = [load(r) for r in range(-1, count + 1)]
    pairs = [[a + b for a, b in zip(values[r], values[r + 1])] for r in range(count + 1)]
    for r in range(count):
        column = [a + b for a, b in zip(pairs[r], pairs[r + 1])]
        from_left = pltpu.roll(column[STEPS - 1], 1, 1)
        from_right = pltpu.roll(column[0], 127, 1)
        across = [column[s] + column[s + 1] for s in range(STEPS - 1)]
        both = [(from_left + column[0]) + across[0]]
        both += [across[s - 1] + across[s] for s in range(1, STEPS - 1)]
        both.append(across[STEPS - 2] + (column[STEPS - 1] + from_right))
        for step in range(STEPS):
            moved = mask(step, r) * both[step]
            value = values[r + 1][step]
            if first:
                new = 0.5 * moved - value
            else:
                new = (moved - (value + value)) - terms[past, plane, step, rows(origin + 2 * ahead + r), :]
            terms[now + 1, plane, step, rows(origin + r), :] = new


def combine(terms, table, place, rows, step, orders):
    total = [None] * 4
    for order in range(orders):
        re = jnp.take_along_axis(jnp.broadcast_to(table[order, :][None], (8, 128)), place, axis=1)
        im = jnp.take_along_axis(jnp.broadcast_to(table[orders + order, :][None], (8, 128)), place, axis=1)
        for waves in (0, 2):
            real = terms[order, waves, step, rows(order), :]
            imag = terms[order, waves + 1, step, rows(order), :]
            if waves == 0:
                new = (re * real - im * imag, re * imag + im * real)
            else:
                new = (re * real + im * imag, re * imag - im * real)
            for part in range(2):
                old = total[waves + part]
                total[waves + part] = new[part] if old is None else old + new[part]
    return total


def column_mask(shape, step, flags):
    column = (lax.broadcasted_iota(jnp.int32, shape, 1) % 64) * STEPS + step
    return 0.25 * jnp.where(column < SIDE, flags[2], jnp.where(column >= SIDE + COLS, flags[3], 1.0))


def inner_kernel(
    flags, fields, indices0, indices1, table, spread, strips0, strips1, picture, inner_source, inner_receiver,
    terms, fresh, masks, places, result,
):
    orders = terms.shape[0]
    for plane in range(4):
        for step in range(STEPS):
            terms[0, plane, step, :ROWS, :] = fields[plane, step]
    for step in range(STEPS):
        places[0, step] = indices0[step].astype(jnp.int32)
        places[1, step] = indices1[step].astype(jnp.int32)
        masks[step] = column_mask((8, 128), step, flags)

    def mask(step, r):
        return masks[step]

    for depth in range(2):
        height = ROWS - 2 * HALF * depth
        for first, last in ((0, 1), (1, 3), (3, 7), (7, 11), (11, 12)):
            count = -(-(height - 2 * (first + 1)) // 8)
            count += count == 8

            def step_on(at, carry, first=first, count=count):
                past, pair = lax.div(at, 2), lax.rem(at, 2)
                for plane in range(2):
                    advance(terms, past, 2 * pair + plane, 0, 1, count, mask, first == 0)
                return carry

            start = max(first - 1, 0)
            lax.fori_loop(2 * start, 2 * (start + last - first), step_on, 0)

        strips = (strips0, strips1)[depth]

        def hand_over(order, carry, strips=strips, height=height):
            for plane in range(4):
                for step in range(STEPS):
                    strips[order, plane, step, :STRIP, :] = terms[order, plane, step, :STRIP, :]
                    strips[order, plane, step, STRIP:, :] = terms[order, plane, step, pl.ds(height - STRIP - 2 * order, STRIP), :]
            return carry

        lax.fori_loop(0, orders, hand_over, 0)
        first_row = HALF * (depth + 1)
        count = (ROWS - 2 * first_row) // 8

        def gather(r, carry, depth=depth, first_row=first_row, count=count):
            own_rows = pl.ds(first_row + r, 8, stride=count)
            for step in range(STEPS):
                place = places[depth, step, own_rows, :]
                total = combine(terms, table, place, lambda k: pl.ds(HALF - k + r, 8, stride=count), step, orders)
                for plane in range(4):
                    fresh[plane, step, pl.ds(r, 8, stride=count), :] = total[plane]
                picture[depth, step, own_rows, :] = total[0] * total[2] + total[1] * total[3]
            return carry

        lax.fori_loop(0, count, gather, 0)
        for plane in range(4):
            for step in range(STEPS):
                piece = fresh[plane, step, : 8 * count, :]
                if depth == 0:
                    terms[0, plane, step, : 8 * count, :] = piece
                else:
                    result[plane * 8 * count : (plane + 1) * 8 * count, step * 128 : (step + 1) * 128] = piece

    size = ROWS - 2 * HALO
    values = exact_dot(result[...], spread[: 2 * COLS, :], ((1,), (1,)))
    for plane in range(4):
        out = (inner_source, inner_receiver)[plane // 2]
        for wave in range(2):
            out[plane % 2, wave] = values[plane * size : (plane + 1) * size, wave * COLS : (wave + 1) * COLS]


def rim_kernel(
    flags, fields, indices0, indices1, above, below, strips0, strips1, inner_picture, inner_source, inner_receiver,
    table, spread, source_out, receiver_out, image, upper, lower, fresh, masks, places, picture, result,
):
    orders = upper.shape[0]
    for plane in range(4):
        for step in range(STEPS):
            at = (plane * STEPS + step) * HALO
            upper[0, plane, step, :HALO, :] = above[at : at + HALO, :]
            upper[0, plane, step, HALO:, :] = fields[plane, step, :STRIP, :]
            lower[0, plane, step, :STRIP, :] = fields[plane, step, ROWS - STRIP :, :]
            lower[0, plane, step, STRIP:, :] = below[at : at + HALO, :]
    for step in range(STEPS):
        at = FIELD_ROWS + step * INDEX_HALO
        places[0, 0, step, :INDEX_HALO, :] = above[at : at + INDEX_HALO, :].astype(jnp.int32)
        places[0, 0, step, INDEX_HALO:, :] = indices0[step, :INDEX_HALO, :].astype(jnp.int32)
        places[0, 1, step, :INDEX_HALO, :] = indices0[step, ROWS - INDEX_HALO :, :].astype(jnp.int32)
        places[0, 1, step, INDEX_HALO:, :] = below[at : at + INDEX_HALO, :].astype(jnp.int32)
        places[1, 0, step] = indices1[step, : 2 * INDEX_HALO, :].astype(jnp.int32)
        places[1, 1, step] = indices1[step, ROWS - 2 * INDEX_HALO :, :].astype(jnp.int32)
        masks[step] = column_mask((8, 128), step, flags)
        for depth in range(2):
            picture[depth, step, OFFSET : OFFSET + ROWS, :] = inner_picture[depth, step]

    width = HALO // 8
    sublane = lax.broadcasted_iota(jnp.int32, (8, 128), 0) * width
    for depth in range(2):
        strips = (strips0, strips1)[depth]
        if depth == 1:
            for plane in range(4):
                for step in range(STEPS):
                    upper[0, plane, step, :HALO, :] = fresh[0, plane, step]
                    upper[0, plane, step, HALO:, :] = strips[0, plane, step, :STRIP, :]
                    lower[0, plane, step, :STRIP, :] = strips[0, plane, step, STRIP:, :]
                    lower[0, plane, step, STRIP:, :] = fresh[1, plane, step]

        def step_on(past, carry, first, depth=depth, strips=strips):
            order = 1 if first else past + 2
            shift = order - HALO + HALF * depth
            inside_upper = [jnp.where(sublane + (r + shift) >= 0, 1.0, flags[0]) for r in range(width)]
            inside_lower = [jnp.where(sublane + (r - HALO - shift) < 0, 1.0, flags[1]) for r in range(width)]
            for plane in range(4):
                for step in range(STEPS):
                    upper[order, plane, step, HALO:, :] = strips[order, plane, step, :STRIP, :]
                    lower[order, plane, step, :STRIP, :] = strips[order, plane, step, STRIP:, :]
                advance(upper, past, plane, 0, 1, width, lambda step, r: inside_upper[r] * masks[step], first)
                advance(lower, past, plane, STRIP, -1, width, lambda step, r: inside_lower[r] * masks[step], first)
            return carry

        step_on(0, 0, True)
        lax.fori_loop(0, orders - 2, lambda past, carry: step_on(past, carry, False), 0)

        def gather(r, carry, depth=depth):
            for side, terms in enumerate((upper, lower)):
                ahead, start = ((-1, HALF), (1, STRIP - HALF))[side]
                in_places = ((4, 4), (0, 8))[depth][side]
                in_picture = OFFSET + (-HALF + HALF * depth, ROWS - HALF - HALF * depth)[side]
                for step in range(STEPS):
                    place = places[depth, side, step, pl.ds(in_places + r, 8, stride=width), :]
                    total = combine(
                        terms, table, place, lambda k: pl.ds(start + ahead * k + r, 8, stride=width), step, orders
                    )
                    for plane in range(4):
                        fresh[side, plane, step, pl.ds(r, 8, stride=width), :] = total[plane]
                    picture[depth, step, pl.ds(in_picture + r, 8, stride=width), :] = total[0] * total[2] + total[1] * total[3]
            return carry

        lax.fori_loop(0, width, gather, 0)

    for step in range(STEPS):
        cut = slice(step * 128, (step + 1) * 128)
        for plane in range(4):
            at = 2 * HALO * plane
            result[at : at + HALO, cut] = fresh[0, plane, step]
            result[at + HALO : at + 2 * HALO, cut] = fresh[1, plane, step]
        for depth in range(2):
            at = 8 * HALO + ROWS * depth
            result[at : at + ROWS, cut] = picture[depth, step, OFFSET : OFFSET + ROWS, :]
    values = exact_dot(result[...], spread[: 2 * COLS, :], ((1,), (1,)))
    for plane in range(4):
        out = (source_out, receiver_out)[plane // 2]
        inner = (inner_source, inner_receiver)[plane // 2]
        at = 2 * HALO * plane
        for wave in range(2):
            cut = slice(wave * COLS, (wave + 1) * COLS)
            out[plane % 2, wave, :HALO] = values[at : at + HALO, cut]
            out[plane % 2, wave, INNER] = inner[plane % 2, wave]
            out[plane % 2, wave, ROWS - HALO :] = values[at + HALO : at + 2 * HALO, cut]
    for depth in range(2):
        at = 8 * HALO + ROWS * depth
        total = values[at : at + ROWS, :COLS] + values[at : at + ROWS, COLS:]
        for part in range(8):
            image[part, depth] = total[part * 8 : (part + 1) * 8]


def full(count):
    return [pl.BlockSpec(memory_space=pltpu.VMEM)] * count


def shape(*dims, dtype=jnp.float32):
    return jax.ShapeDtypeStruct(dims, dtype)


def params(megabytes):
    return pltpu.CompilerParams(vmem_limit_bytes=megabytes * 1024 * 1024)


def cost(flops):
    return pl.CostEstimate(flops=flops, bytes_accessed=2**20, transcendentals=0)


def shift(block, axis, forward):
    count = lax.axis_size(axis)
    pairs = [(i, i + 1) for i in range(count - 1)]
    return lax.ppermute(block, axis, pairs if forward else [(b, a) for a, b in pairs])


def extrapolate(source, receiver, table_index, coef_table):
    orders = coef_table.shape[2]
    spread = spread_matrix()
    at_x, at_y = lax.axis_index("sx"), lax.axis_index("sy")
    flags = jnp.stack(
        [at_x > 0, at_x < lax.axis_size("sx") - 1, at_y > 0, at_y < lax.axis_size("sy") - 1]
    ).astype(jnp.float32)
    table = jnp.pad(jnp.swapaxes(coef_table, 1, 2).reshape(2 * orders, -1), ((0, 0), (0, 128 - coef_table.shape[1])))
    scalars = [pl.BlockSpec(memory_space=pltpu.SMEM)]

    left, right = pl.pallas_call(
        edges_kernel,
        out_shape=(shape(3, ROWS, 128), shape(3, ROWS, 128)),
        in_specs=[pl.BlockSpec(memory_space=pltpu.HBM)] * 3,
        out_specs=tuple(full(2)),
        scratch_shapes=[
            pltpu.VMEM((2, 2, 2, ROWS, COLS), jnp.float32),
            pltpu.VMEM((2, ROWS, COLS), jnp.int32),
            pltpu.SemaphoreType.DMA((3,)),
        ],
        compiler_params=params(56),
        name="edges",
    )(source, receiver, table_index)
    low = shift(right, "sy", True)
    high = shift(left, "sy", False)
    own, indices = pl.pallas_call(
        own_kernel,
        out_shape=(shape(4, STEPS, ROWS, 128), shape(2, STEPS, ROWS, 128)),
        in_specs=full(4),
        out_specs=tuple(full(2)),
        scratch_shapes=[pltpu.VMEM((ROWS, 2 * COLS), jnp.float32)],
        compiler_params=params(16),
        cost_estimate=cost(2 * 10**9),
        name="own",
    )(source, receiver, table_index, spread)
    fields, indices0, top, bottom = pl.pallas_call(
        merge_kernel,
        out_shape=(shape(4, STEPS, ROWS, 128), shape(STEPS, ROWS, 128), shape(SEND, 128), shape(SEND, 128)),
        in_specs=full(5),
        out_specs=tuple(full(4)),
        scratch_shapes=[pltpu.VMEM((5 * ROWS, 128), jnp.float32)],
        compiler_params=params(16),
        name="merge",
    )(own, indices, low, high, spread)
    indices1 = indices[1]
    above = shift(bottom, "sx", True)
    below = shift(top, "sx", False)
    strip = shape(orders, 4, STEPS, 2 * STRIP, 128)
    strips0, strips1, picture, inner_source, inner_receiver = pl.pallas_call(
        inner_kernel,
        out_shape=(
            strip,
            strip,
            shape(2, STEPS, ROWS, 128),
            shape(2, 2, ROWS - 2 * HALO, COLS),
            shape(2, 2, ROWS - 2 * HALO, COLS),
        ),
        in_specs=scalars + full(5),
        out_specs=tuple(full(5)),
        scratch_shapes=[
            pltpu.VMEM((orders, 4, STEPS, ROWS + 16, 128), jnp.float32),
            pltpu.VMEM((4, STEPS, ROWS - HALO, 128), jnp.float32),
            pltpu.VMEM((STEPS, 8, 128), jnp.float32),
            pltpu.VMEM((2, STEPS, ROWS, 128), jnp.int32),
            pltpu.VMEM((4 * (ROWS - 2 * HALO), WIDE), jnp.float32),
        ],
        compiler_params=params(32),
        cost_estimate=cost(10**10),
        name="inner",
    )(flags, fields, indices0, indices1, table, spread)
    return pl.pallas_call(
        rim_kernel,
        out_shape=(shape(2, 2, ROWS, COLS), shape(2, 2, ROWS, COLS), shape(8, 2, 8, COLS)),
        in_specs=scalars + full(12),
        out_specs=tuple(full(3)),
        scratch_shapes=[
            pltpu.VMEM((orders, 4, STEPS, HALO + STRIP, 128), jnp.float32),
            pltpu.VMEM((orders, 4, STEPS, HALO + STRIP, 128), jnp.float32),
            pltpu.VMEM((2, 4, STEPS, HALO, 128), jnp.float32),
            pltpu.VMEM((STEPS, 8, 128), jnp.float32),
            pltpu.VMEM((2, 2, STEPS, 2 * INDEX_HALO, 128), jnp.int32),
            pltpu.VMEM((2, STEPS, TALL, 128), jnp.float32),
            pltpu.VMEM((8 * HALO + 2 * ROWS, WIDE), jnp.float32),
        ],
        compiler_params=params(32),
        name="rim",
    )(flags, fields, indices0, indices1, above, below, strips0, strips1, picture, inner_source, inner_receiver, table, spread)


def add_over_freq(pieces):
    groups = [[y * 4 + z * 2 + core for y in range(4) for core in range(2)] for z in range(2)]
    mine = jnp.sum(lax.all_to_all(pieces, "freq", 0, 0, axis_index_groups=groups), axis=0)
    mine = mine + lax.ppermute(mine, "freq", [(i, i ^ 2) for i in range(16)])
    blocks = lax.all_to_all(jnp.broadcast_to(mine[None], pieces.shape), "freq", 0, 0, axis_index_groups=groups)
    return jnp.swapaxes(blocks, 0, 1).reshape(2, ROWS, COLS)


def local(source, receiver, table_index, coef_table):
    source_out, receiver_out, pieces = extrapolate(source, receiver, table_index, coef_table)
    return source_out, receiver_out, add_over_freq(pieces)


def solution(mesh):
    placed = P(None, "freq", "sx", "sy")
    return jax.shard_map(
        local,
        mesh=mesh,
        in_specs=(placed, placed, placed, P()),
        out_specs=(placed, placed, P(None, "sx", "sy")),
        check_vma=False,
    )
```

```python
import jax
import jax.numpy as jnp
from jax import lax
from jax.experimental import pallas as pl
from jax.experimental.pallas import tpu as pltpu
from jax.sharding import PartitionSpec as P

ROWS, COLS = 64, 256
HALO = 24
HALF = HALO // 2
SIDE = 32
STEPS = 5
INDEX_HALO = 16
FIELD_ROWS = 4 * STEPS * HALO
SEND = FIELD_ROWS + STEPS * INDEX_HALO
WIDE = STEPS * 128
STRIP = 16
OFFSET = 32
TALL = 128
BLOCK = 16


def fill_spread(spread):
    lane = lax.broadcasted_iota(jnp.int32, (128, 128), 1)
    row = lax.broadcasted_iota(jnp.int32, (128, 128), 0)
    for part in range(STEPS):
        if part < 4:
            wave, column = part // 2, SIDE + (part % 2) * 128 + row
        else:
            wave = lax.rem(lax.div(row, SIDE), 2)
            column = lax.rem(row, SIDE) + jnp.where(row < 2 * SIDE, 0, SIDE + COLS)
        goes = wave * 512 + column
        for step in range(STEPS):
            place = lax.div(lane, 64) * 512 + lax.rem(lane, 64) * STEPS + step
            here = jnp.where(goes == place, 1.0, 0.0).astype(jnp.bfloat16)
            spread[part * 128 : (part + 1) * 128, step * 128 : (step + 1) * 128] = here


def dot(left, right, contract):
    return lax.dot_general(left, right, (contract, ((), ())), preferred_element_type=jnp.float32)


def move(left, right, contract):
    high = left.astype(jnp.bfloat16)
    low = (left - high.astype(jnp.float32)).astype(jnp.bfloat16)
    return dot(high, right, contract) + dot(low, right, contract)


def edges_kernel(source, receiver, index, left, right, waves, places, sems):
    copies = [
        [
            pltpu.make_async_copy(field.at[part, wave], waves.at[kind, part, wave], sems.at[kind, 2 * part + wave])
            for part in range(2)
            for wave in range(2)
        ]
        for kind, field in enumerate((source, receiver))
    ]
    copies.append([pltpu.make_async_copy(index.at[depth], places.at[depth], sems.at[2, depth]) for depth in range(2)])
    for copy in sum(copies, []):
        copy.start()
    lane = lax.broadcasted_iota(jnp.int32, (ROWS, 128), 1)

    def join(parts, start):
        total = jnp.zeros((ROWS, 128), jnp.float32)
        for place, part in enumerate(parts):
            shift = (place * SIDE - start) % 128
            moved = part if shift == 0 else pltpu.roll(part, shift, 1)
            total = jnp.where((lane >= place * SIDE) & (lane < (place + 1) * SIDE), moved, total)
        return total

    ends = ((right, 1, 128 - SIDE), (left, 0, 0))
    for kind in range(3):
        for copy in copies[kind]:
            copy.wait()
        for out, tile, start in ends:
            cut = slice(tile * 128, (tile + 1) * 128)
            if kind < 2:
                out[kind] = join([waves[kind, part, wave, :, cut] for part in range(2) for wave in range(2)], start)
            else:
                out[2] = join([places[0, wave, :, cut].astype(jnp.float32) for wave in range(2)], start)


def own_kernel(waves, index, fields, indices, spread, joined):
    fill_spread(spread)
    matrix = spread[: 2 * COLS, :]
    for plane in range(6):
        for wave in range(2):
            cut = slice(wave * COLS, (wave + 1) * COLS)
            if plane < 4:
                joined[:, cut] = waves[plane // 2, plane % 2, wave]
            else:
                joined[:, cut] = index[plane - 4, wave].astype(jnp.float32)
        if plane < 4:
            values = move(joined[...], matrix, ((1,), (0,)))
        else:
            values = dot(joined[...].astype(jnp.bfloat16), matrix, ((1,), (0,)))
        for step in range(STEPS):
            piece = values[:, step * 128 : (step + 1) * 128]
            if plane < 4:
                fields[plane, step] = piece
            else:
                indices[plane - 4, step] = piece


def merge_kernel(own, indices, low, high, spread, fields, indices0, top, bottom, joined):
    lane = lax.broadcasted_iota(jnp.int32, (ROWS, 128), 1)
    matrix = spread[2 * COLS :, :]
    for plane in range(5):
        from_low, from_high = low[plane // 2], high[plane // 2]
        if plane % 2 == 0:
            from_high = pltpu.roll(from_high, 64, 1)
        else:
            from_low = pltpu.roll(from_low, 64, 1)
        joined[plane * ROWS : (plane + 1) * ROWS, :] = jnp.where(lane < 64, from_low, from_high)
    values = move(joined[...], matrix, ((1,), (0,)))
    for plane in range(5):
        for step in range(STEPS):
            piece = values[plane * ROWS : (plane + 1) * ROWS, step * 128 : (step + 1) * 128]
            if plane < 4:
                piece = piece + own[plane, step]
                fields[plane, step] = piece
                rows, at = HALO, (plane * STEPS + step) * HALO
            else:
                piece = piece + indices[0, step]
                indices0[step] = piece
                rows, at = INDEX_HALO, FIELD_ROWS + step * INDEX_HALO
            top[at : at + rows, :] = piece[:rows]
            bottom[at : at + rows, :] = piece[ROWS - rows :]


def advance(terms, past, plane, origin, ahead, count, mask, first):
    now = 0 if first else past + 1

    def rows(first_row):
        return pl.ds(first_row, 8, stride=count)

    def load(r):
        return [terms[now, plane, step, rows(origin + ahead + r), :] for step in range(STEPS)]

    values = [load(r) for r in range(-1, count + 1)]
    pairs = [[a + b for a, b in zip(values[r], values[r + 1])] for r in range(count + 1)]
    for r in range(count):
        column = [a + b for a, b in zip(pairs[r], pairs[r + 1])]
        from_left = pltpu.roll(column[STEPS - 1], 1, 1)
        from_right = pltpu.roll(column[0], 127, 1)
        across = [column[s] + column[s + 1] for s in range(STEPS - 1)]
        both = [(from_left + column[0]) + across[0]]
        both += [across[s - 1] + across[s] for s in range(1, STEPS - 1)]
        both.append(across[STEPS - 2] + (column[STEPS - 1] + from_right))
        for step in range(STEPS):
            moved = mask(step, r) * both[step]
            value = values[r + 1][step]
            if first:
                new = 0.5 * moved - value
            else:
                new = (moved - (value + value)) - terms[past, plane, step, rows(origin + 2 * ahead + r), :]
            terms[now + 1, plane, step, rows(origin + r), :] = new


def combine(terms, table, place, rows, step, orders):
    total = [None] * 4
    for order in range(orders):
        re = jnp.take_along_axis(jnp.broadcast_to(table[order, :][None], (8, 128)), place, axis=1)
        im = jnp.take_along_axis(jnp.broadcast_to(table[orders + order, :][None], (8, 128)), place, axis=1)
        for waves in (0, 2):
            real = terms[order, waves, step, rows(order), :]
            imag = terms[order, waves + 1, step, rows(order), :]
            if waves == 0:
                new = (re * real - im * imag, re * imag + im * real)
            else:
                new = (re * real + im * imag, re * imag - im * real)
            for part in range(2):
                old = total[waves + part]
                total[waves + part] = new[part] if old is None else old + new[part]
    return total


def fill(lookup, table):
    orders, parts, entries = table.shape
    lookup[...] = jnp.zeros(lookup.shape, jnp.float32)
    for order in range(orders):
        for part in range(parts):
            at = part * orders + order
            lookup[at : at + 1, :entries] = table[order, part : part + 1, :]


def column_mask(shape, step, flags):
    column = (lax.broadcasted_iota(jnp.int32, shape, 1) % 64) * STEPS + step
    return 0.25 * jnp.where(column < SIDE, flags[2], jnp.where(column >= SIDE + COLS, flags[3], 1.0))


def inner_kernel(
    flags, fields, indices0, indices1, table, strips0, strips1, picture, centre,
    terms, fresh, masks, places, lookup,
):
    orders = terms.shape[0]
    fill(lookup, table)
    for plane in range(4):
        for step in range(STEPS):
            terms[0, plane, step, :ROWS, :] = fields[plane, step]
    for step in range(STEPS):
        places[0, step] = indices0[step].astype(jnp.int32)
        places[1, step] = indices1[step].astype(jnp.int32)
        masks[step] = column_mask((8, 128), step, flags)

    def mask(step, r):
        return masks[step]

    for depth in range(2):
        height = ROWS - 2 * HALF * depth
        for first, last in ((0, 1), (1, 3), (3, 7), (7, 11), (11, 12)):
            count = -(-(height - 2 * (first + 1)) // 8)
            count += count == 8

            def step_on(at, carry, first=first, count=count):
                past, pair = lax.div(at, 2), lax.rem(at, 2)
                for plane in range(2):
                    advance(terms, past, 2 * pair + plane, 0, 1, count, mask, first == 0)
                return carry

            start = max(first - 1, 0)
            lax.fori_loop(2 * start, 2 * (start + last - first), step_on, 0)

        strips = (strips0, strips1)[depth]

        def hand_over(order, carry, strips=strips, height=height):
            for plane in range(4):
                for step in range(STEPS):
                    strips[order, plane, step, :STRIP, :] = terms[order, plane, step, :STRIP, :]
                    strips[order, plane, step, STRIP:, :] = terms[order, plane, step, pl.ds(height - STRIP - 2 * order, STRIP), :]
            return carry

        lax.fori_loop(0, orders, hand_over, 0)
        first_row = HALF * (depth + 1)
        count = (ROWS - 2 * first_row) // 8

        def gather(r, carry, depth=depth, first_row=first_row, count=count):
            own_rows = pl.ds(first_row + r, 8, stride=count)
            for step in range(STEPS):
                place = places[depth, step, own_rows, :]
                total = combine(terms, lookup, place, lambda k: pl.ds(HALF - k + r, 8, stride=count), step, orders)
                for plane in range(4):
                    fresh[plane, step, pl.ds(r, 8, stride=count), :] = total[plane]
                picture[depth, step, own_rows, :] = total[0] * total[2] + total[1] * total[3]
            return carry

        lax.fori_loop(0, count, gather, 0)
        for plane in range(4):
            for step in range(STEPS):
                piece = fresh[plane, step, : 8 * count, :]
                if depth == 0:
                    terms[0, plane, step, : 8 * count, :] = piece
                else:
                    centre[plane, step] = piece


def rim_kernel(
    flags, fields, indices0, indices1, above, below, strips0, strips1, inner_picture, table, spread, fresh, image,
    upper, lower, masks, places, picture, result, lookup,
):
    orders = upper.shape[0]
    fill(lookup, table)
    for plane in range(4):
        for step in range(STEPS):
            at = (plane * STEPS + step) * HALO
            upper[0, plane, step, :HALO, :] = above[at : at + HALO, :]
            upper[0, plane, step, HALO:, :] = fields[plane, step, :STRIP, :]
            lower[0, plane, step, :STRIP, :] = fields[plane, step, ROWS - STRIP :, :]
            lower[0, plane, step, STRIP:, :] = below[at : at + HALO, :]
    for step in range(STEPS):
        at = FIELD_ROWS + step * INDEX_HALO
        places[0, 0, step, :INDEX_HALO, :] = above[at : at + INDEX_HALO, :].astype(jnp.int32)
        places[0, 0, step, INDEX_HALO:, :] = indices0[step, :INDEX_HALO, :].astype(jnp.int32)
        places[0, 1, step, :INDEX_HALO, :] = indices0[step, ROWS - INDEX_HALO :, :].astype(jnp.int32)
        places[0, 1, step, INDEX_HALO:, :] = below[at : at + INDEX_HALO, :].astype(jnp.int32)
        places[1, 0, step] = indices1[step, : 2 * INDEX_HALO, :].astype(jnp.int32)
        places[1, 1, step] = indices1[step, ROWS - 2 * INDEX_HALO :, :].astype(jnp.int32)
        masks[step] = column_mask((8, 128), step, flags)
        for depth in range(2):
            picture[depth, step, OFFSET : OFFSET + ROWS, :] = inner_picture[depth, step]

    width = HALO // 8
    sublane = lax.broadcasted_iota(jnp.int32, (8, 128), 0) * width
    for depth in range(2):
        strips = (strips0, strips1)[depth]
        if depth == 1:
            for plane in range(4):
                for step in range(STEPS):
                    upper[0, plane, step, :HALO, :] = fresh[0, plane, step]
                    upper[0, plane, step, HALO:, :] = strips[0, plane, step, :STRIP, :]
                    lower[0, plane, step, :STRIP, :] = strips[0, plane, step, STRIP:, :]
                    lower[0, plane, step, STRIP:, :] = fresh[1, plane, step]

        def step_on(past, carry, first, depth=depth, strips=strips):
            order = 1 if first else past + 2
            shift = order - HALO + HALF * depth
            inside_upper = [jnp.where(sublane + (r + shift) >= 0, 1.0, flags[0]) for r in range(width)]
            inside_lower = [jnp.where(sublane + (r - HALO - shift) < 0, 1.0, flags[1]) for r in range(width)]
            for plane in range(4):
                for step in range(STEPS):
                    upper[order, plane, step, HALO:, :] = strips[order, plane, step, :STRIP, :]
                    lower[order, plane, step, :STRIP, :] = strips[order, plane, step, STRIP:, :]
                advance(upper, past, plane, 0, 1, width, lambda step, r: inside_upper[r] * masks[step], first)
                advance(lower, past, plane, STRIP, -1, width, lambda step, r: inside_lower[r] * masks[step], first)
            return carry

        step_on(0, 0, True)
        lax.fori_loop(0, orders - 2, lambda past, carry: step_on(past, carry, False), 0)

        def gather(r, carry, depth=depth):
            for side, terms in enumerate((upper, lower)):
                ahead, start = ((-1, HALF), (1, STRIP - HALF))[side]
                in_places = ((4, 4), (0, 8))[depth][side]
                in_picture = OFFSET + (-HALF + HALF * depth, ROWS - HALF - HALF * depth)[side]
                for step in range(STEPS):
                    place = places[depth, side, step, pl.ds(in_places + r, 8, stride=width), :]
                    total = combine(
                        terms, lookup, place, lambda k: pl.ds(start + ahead * k + r, 8, stride=width), step, orders
                    )
                    for plane in range(4):
                        fresh[side, plane, step, pl.ds(r, 8, stride=width), :] = total[plane]
                    picture[depth, step, pl.ds(in_picture + r, 8, stride=width), :] = total[0] * total[2] + total[1] * total[3]
            return carry

        lax.fori_loop(0, width, gather, 0)

    for step in range(STEPS):
        for depth in range(2):
            piece = picture[depth, step, OFFSET : OFFSET + ROWS, :]
            result[depth * ROWS : (depth + 1) * ROWS, step * 128 : (step + 1) * 128] = piece
    values = move(result[...], spread[: 2 * COLS, :], ((1,), (1,)))
    total = values[:, :COLS] + values[:, COLS:]
    for part in range(8):
        image[part] = total[part * BLOCK : (part + 1) * BLOCK]


def finish_kernel(fresh, centre, spread, source_out, receiver_out, result):
    for plane in range(4):
        for step in range(STEPS):
            rows, cut = plane * ROWS, slice(step * 128, (step + 1) * 128)
            result[rows : rows + HALO, cut] = fresh[0, plane, step]
            result[rows + HALO : rows + ROWS - HALO, cut] = centre[plane, step]
            result[rows + ROWS - HALO : rows + ROWS, cut] = fresh[1, plane, step]
    values = move(result[...], spread[: 2 * COLS, :], ((1,), (1,)))
    for plane in range(4):
        for wave in range(2):
            piece = values[plane * ROWS : (plane + 1) * ROWS, wave * COLS : (wave + 1) * COLS]
            (source_out, receiver_out)[plane // 2][plane % 2, wave] = piece


def full(count):
    return [pl.BlockSpec(memory_space=pltpu.VMEM)] * count


def shape(*dims, dtype=jnp.float32):
    return jax.ShapeDtypeStruct(dims, dtype)


def params(megabytes):
    return pltpu.CompilerParams(vmem_limit_bytes=megabytes * 1024 * 1024)


def cost(flops):
    return pl.CostEstimate(flops=flops, bytes_accessed=2**20, transcendentals=0)


def shift(block, axis, forward):
    count = lax.axis_size(axis)
    pairs = [(i, i + 1) for i in range(count - 1)]
    return lax.ppermute(block, axis, pairs if forward else [(b, a) for a, b in pairs])


def extrapolate(source, receiver, table_index, coef_table):
    orders = coef_table.shape[2]
    at_x, at_y = lax.axis_index("sx"), lax.axis_index("sy")
    flags = jnp.stack(
        [at_x > 0, at_x < lax.axis_size("sx") - 1, at_y > 0, at_y < lax.axis_size("sy") - 1]
    ).astype(jnp.float32)
    table = jnp.transpose(coef_table, (2, 0, 1))
    scalars = [pl.BlockSpec(memory_space=pltpu.SMEM)]

    left, right, waves, places = pl.pallas_call(
        edges_kernel,
        out_shape=(
            pltpu.VMEM((3, ROWS, 128), jnp.float32),
            pltpu.VMEM((3, ROWS, 128), jnp.float32),
            pltpu.VMEM((2, 2, 2, ROWS, COLS), jnp.float32),
            pltpu.VMEM((2, 2, ROWS, COLS), jnp.int32),
        ),
        in_specs=[pl.BlockSpec(memory_space=pltpu.HBM)] * 3,
        out_specs=tuple(full(4)),
        scratch_shapes=[pltpu.SemaphoreType.DMA((3, 4))],
        compiler_params=params(16),
        name="edges",
    )(*(pltpu.with_memory_space_constraint(array, pltpu.HBM) for array in (source, receiver, table_index)))
    low = shift(right, "sy", True)
    high = shift(left, "sy", False)
    own, indices, spread = pl.pallas_call(
        own_kernel,
        out_shape=(shape(4, STEPS, ROWS, 128), shape(2, STEPS, ROWS, 128), shape(WIDE, WIDE, dtype=jnp.bfloat16)),
        in_specs=full(2),
        out_specs=tuple(full(3)),
        scratch_shapes=[pltpu.VMEM((ROWS, 2 * COLS), jnp.float32)],
        compiler_params=params(16),
        cost_estimate=cost(2 * 10**9),
        name="own",
    )(waves, places)
    fields, indices0, top, bottom = pl.pallas_call(
        merge_kernel,
        out_shape=(shape(4, STEPS, ROWS, 128), shape(STEPS, ROWS, 128), shape(SEND, 128), shape(SEND, 128)),
        in_specs=full(5),
        out_specs=tuple(full(4)),
        scratch_shapes=[pltpu.VMEM((5 * ROWS, 128), jnp.float32)],
        compiler_params=params(16),
        name="merge",
    )(own, indices, low, high, spread)
    indices1 = indices[1]
    above = shift(bottom, "sx", True)
    below = shift(top, "sx", False)
    strip = shape(orders, 4, STEPS, 2 * STRIP, 128)
    lookup = pltpu.VMEM((2 * orders, 128), jnp.float32)
    strips0, strips1, picture, centre = pl.pallas_call(
        inner_kernel,
        out_shape=(strip, strip, shape(2, STEPS, ROWS, 128), shape(4, STEPS, ROWS - 2 * HALO, 128)),
        in_specs=scalars + full(4),
        out_specs=tuple(full(4)),
        scratch_shapes=[
            pltpu.VMEM((orders, 4, STEPS, ROWS + 16, 128), jnp.float32),
            pltpu.VMEM((4, STEPS, ROWS - HALO, 128), jnp.float32),
            pltpu.VMEM((STEPS, 8, 128), jnp.float32),
            pltpu.VMEM((2, STEPS, ROWS, 128), jnp.int32),
            lookup,
        ],
        compiler_params=params(32),
        cost_estimate=cost(10**10),
        name="inner",
    )(flags, fields, indices0, indices1, table)
    fresh, image = pl.pallas_call(
        rim_kernel,
        out_shape=(shape(2, 4, STEPS, HALO, 128), shape(8, BLOCK, COLS)),
        in_specs=scalars + full(10),
        out_specs=tuple(full(2)),
        scratch_shapes=[
            pltpu.VMEM((orders, 4, STEPS, HALO + STRIP, 128), jnp.float32),
            pltpu.VMEM((orders, 4, STEPS, HALO + STRIP, 128), jnp.float32),
            pltpu.VMEM((STEPS, 8, 128), jnp.float32),
            pltpu.VMEM((2, 2, STEPS, 2 * INDEX_HALO, 128), jnp.int32),
            pltpu.VMEM((2, STEPS, TALL, 128), jnp.float32),
            pltpu.VMEM((2 * ROWS, WIDE), jnp.float32),
            lookup,
        ],
        compiler_params=params(32),
        name="rim",
    )(flags, fields, indices0, indices1, above, below, strips0, strips1, picture, table, spread)
    source_out, receiver_out = pl.pallas_call(
        finish_kernel,
        out_shape=(shape(2, 2, ROWS, COLS), shape(2, 2, ROWS, COLS)),
        in_specs=full(3),
        out_specs=tuple(full(2)),
        scratch_shapes=[pltpu.VMEM((4 * ROWS, WIDE), jnp.float32)],
        compiler_params=params(16),
        cost_estimate=cost(2 * 10**9),
        name="finish",
    )(fresh, centre, spread)
    return source_out, receiver_out, image


def add_over_freq(pieces):
    groups = [[y * 4 + z * 2 + core for y in range(4) for core in range(2)] for z in range(2)]
    mine = jnp.sum(lax.all_to_all(pieces, "freq", 0, 0, axis_index_groups=groups), axis=0)
    mine = mine + lax.ppermute(mine, "freq", [(i, i ^ 2) for i in range(16)])
    blocks = lax.all_to_all(jnp.broadcast_to(mine[None], pieces.shape), "freq", 0, 0, axis_index_groups=groups)
    return blocks.reshape(2, ROWS, COLS)


def local(source, receiver, table_index, coef_table):
    source_out, receiver_out, pieces = extrapolate(source, receiver, table_index, coef_table)
    return source_out, receiver_out, add_over_freq(pieces)


def solution(mesh):
    placed = P(None, "freq", "sx", "sy")
    return jax.shard_map(
        local,
        mesh=mesh,
        in_specs=(placed, placed, placed, P()),
        out_specs=(placed, placed, P(None, "sx", "sy")),
        check_vma=False,
    )
```

```python
import jax
import jax.numpy as jnp
from jax import lax
from jax.experimental import pallas as pl
from jax.experimental.pallas import tpu as pltpu
from jax.sharding import PartitionSpec as P

ROWS, COLS = 64, 256
HALO = 24
HALF = HALO // 2
SIDE = 32
STEPS = 5
INDEX_HALO = 16
FIELD_ROWS = 4 * STEPS * HALO
SEND = FIELD_ROWS + STEPS * INDEX_HALO
WIDE = STEPS * 128
STRIP = 16
OFFSET = 32
TALL = 128
BLOCK = 16


def fill_spread(spread):
    lane = lax.broadcasted_iota(jnp.int32, (128, 128), 1)
    row = lax.broadcasted_iota(jnp.int32, (128, 128), 0)
    for part in range(STEPS):
        if part < 4:
            wave, column = part // 2, SIDE + (part % 2) * 128 + row
        else:
            wave = lax.rem(lax.div(row, SIDE), 2)
            column = lax.rem(row, SIDE) + jnp.where(row < 2 * SIDE, 0, SIDE + COLS)
        goes = wave * 512 + column
        for step in range(STEPS):
            place = lax.div(lane, 64) * 512 + lax.rem(lane, 64) * STEPS + step
            here = jnp.where(goes == place, 1.0, 0.0).astype(jnp.bfloat16)
            spread[part * 128 : (part + 1) * 128, step * 128 : (step + 1) * 128] = here


def dot(left, right, contract):
    return lax.dot_general(left, right, (contract, ((), ())), preferred_element_type=jnp.float32)


def move(left, right, contract):
    high = left.astype(jnp.bfloat16)
    low = (left - high.astype(jnp.float32)).astype(jnp.bfloat16)
    return dot(high, right, contract) + dot(low, right, contract)


def edges_kernel(source, receiver, index, left, right, waves, places, sems):
    copies = [
        [
            pltpu.make_async_copy(field.at[part, wave], waves.at[kind, part, wave], sems.at[kind, 2 * part + wave])
            for part in range(2)
            for wave in range(2)
        ]
        for kind, field in enumerate((source, receiver))
    ]
    copies.append([pltpu.make_async_copy(index.at[depth], places.at[depth], sems.at[2, depth]) for depth in range(2)])
    for copy in sum(copies, []):
        copy.start()
    lane = lax.broadcasted_iota(jnp.int32, (ROWS, 128), 1)

    def join(parts, start):
        total = jnp.zeros((ROWS, 128), jnp.float32)
        for place, part in enumerate(parts):
            shift = (place * SIDE - start) % 128
            moved = part if shift == 0 else pltpu.roll(part, shift, 1)
            total = jnp.where((lane >= place * SIDE) & (lane < (place + 1) * SIDE), moved, total)
        return total

    ends = ((right, 1, 128 - SIDE), (left, 0, 0))
    for kind in range(3):
        for copy in copies[kind]:
            copy.wait()
        for out, tile, start in ends:
            cut = slice(tile * 128, (tile + 1) * 128)
            if kind < 2:
                out[kind] = join([waves[kind, part, wave, :, cut] for part in range(2) for wave in range(2)], start)
            else:
                out[2] = join([places[0, wave, :, cut].astype(jnp.float32) for wave in range(2)], start)


def own_kernel(waves, index, fields, indices, spread, joined):
    fill_spread(spread)
    matrix = spread[: 2 * COLS, :]
    for plane in range(6):
        for wave in range(2):
            cut = slice(wave * COLS, (wave + 1) * COLS)
            if plane < 4:
                joined[:, cut] = waves[plane // 2, plane % 2, wave]
            else:
                joined[:, cut] = index[plane - 4, wave].astype(jnp.float32)
        if plane < 4:
            values = move(joined[...], matrix, ((1,), (0,)))
        else:
            values = dot(joined[...].astype(jnp.bfloat16), matrix, ((1,), (0,)))
        for step in range(STEPS):
            piece = values[:, step * 128 : (step + 1) * 128]
            if plane < 4:
                fields[plane, step] = piece
            else:
                indices[plane - 4, step] = piece


def merge_kernel(own, indices, low, high, spread, fields, indices0, top, bottom, joined):
    lane = lax.broadcasted_iota(jnp.int32, (ROWS, 128), 1)
    matrix = spread[2 * COLS :, :]
    for plane in range(5):
        from_low, from_high = low[plane // 2], high[plane // 2]
        if plane % 2 == 0:
            from_high = pltpu.roll(from_high, 64, 1)
        else:
            from_low = pltpu.roll(from_low, 64, 1)
        joined[plane * ROWS : (plane + 1) * ROWS, :] = jnp.where(lane < 64, from_low, from_high)
    values = move(joined[...], matrix, ((1,), (0,)))
    for plane in range(5):
        for step in range(STEPS):
            piece = values[plane * ROWS : (plane + 1) * ROWS, step * 128 : (step + 1) * 128]
            if plane < 4:
                piece = piece + own[plane, step]
                fields[plane, step] = piece
                rows, at = HALO, (plane * STEPS + step) * HALO
            else:
                piece = piece + indices[0, step]
                indices0[step] = piece
                rows, at = INDEX_HALO, FIELD_ROWS + step * INDEX_HALO
            top[at : at + rows, :] = piece[:rows]
            bottom[at : at + rows, :] = piece[ROWS - rows :]


def advance(terms, past, plane, origin, ahead, count, mask, first):
    now = 0 if first else past + 1

    def rows(first_row):
        return pl.ds(first_row, 8, stride=count)

    def load(r):
        return [terms[now, plane, step, rows(origin + ahead + r), :] for step in range(STEPS)]

    values = [load(r) for r in range(-1, count + 1)]
    pairs = [[a + b for a, b in zip(values[r], values[r + 1])] for r in range(count + 1)]
    for r in range(count):
        column = [a + b for a, b in zip(pairs[r], pairs[r + 1])]
        from_left = pltpu.roll(column[STEPS - 1], 1, 1)
        from_right = pltpu.roll(column[0], 127, 1)
        across = [column[s] + column[s + 1] for s in range(STEPS - 1)]
        both = [(from_left + column[0]) + across[0]]
        both += [across[s - 1] + across[s] for s in range(1, STEPS - 1)]
        both.append(across[STEPS - 2] + (column[STEPS - 1] + from_right))
        for step in range(STEPS):
            moved = mask(step, r) * both[step]
            value = values[r + 1][step]
            if first:
                new = 0.5 * moved - value
            else:
                new = (moved - (value + value)) - terms[past, plane, step, rows(origin + 2 * ahead + r), :]
            terms[now + 1, plane, step, rows(origin + r), :] = new


def combine(terms, table, place, rows, step, orders):
    total = [None] * 4
    for order in range(orders):
        re = jnp.take_along_axis(jnp.broadcast_to(table[order, :][None], (8, 128)), place, axis=1)
        im = jnp.take_along_axis(jnp.broadcast_to(table[orders + order, :][None], (8, 128)), place, axis=1)
        for waves in (0, 2):
            real = terms[order, waves, step, rows(order), :]
            imag = terms[order, waves + 1, step, rows(order), :]
            if waves == 0:
                new = (re * real - im * imag, re * imag + im * real)
            else:
                new = (re * real + im * imag, re * imag - im * real)
            for part in range(2):
                old = total[waves + part]
                total[waves + part] = new[part] if old is None else old + new[part]
    return total


def fill(lookup, table):
    orders, parts, entries = table.shape
    lookup[...] = jnp.zeros(lookup.shape, jnp.float32)
    for order in range(orders):
        for part in range(parts):
            at = part * orders + order
            lookup[at : at + 1, :entries] = table[order, part : part + 1, :]


def column_mask(shape, step, flags):
    column = (lax.broadcasted_iota(jnp.int32, shape, 1) % 64) * STEPS + step
    return 0.25 * jnp.where(column < SIDE, flags[2], jnp.where(column >= SIDE + COLS, flags[3], 1.0))


def inner_kernel(
    flags, fields, indices0, indices1, table, strips0, strips1, picture, centre,
    terms, fresh, masks, places, lookup,
):
    orders = terms.shape[0]
    fill(lookup, table)
    for plane in range(4):
        for step in range(STEPS):
            terms[0, plane, step, :ROWS, :] = fields[plane, step]
    for step in range(STEPS):
        places[0, step] = indices0[step].astype(jnp.int32)
        places[1, step] = indices1[step].astype(jnp.int32)
        masks[step] = column_mask((8, 128), step, flags)

    def mask(step, r):
        return masks[step]

    for depth in range(2):
        height = ROWS - 2 * HALF * depth
        strips = (strips0, strips1)[depth]

        def hand_over(order, plane, strips=strips, height=height):
            for step in range(STEPS):
                strips[order, plane, step, :STRIP, :] = terms[order, plane, step, :STRIP, :]
                strips[order, plane, step, STRIP:, :] = terms[order, plane, step, pl.ds(height - STRIP - 2 * order, STRIP), :]

        for first, last in ((0, 1), (1, 3), (3, 7), (7, 11), (11, 12)):
            count = -(-(height - 2 * (first + 1)) // 8)
            count += count == 8

            def step_on(past, carry, first=first, count=count, hand_over=hand_over):
                for plane in range(4):
                    hand_over(0 if first == 0 else past + 1, plane)
                for plane in range(4):
                    advance(terms, past, plane, 0, 1, count, mask, first == 0)
                return carry

            start = max(first - 1, 0)
            if last - first == 1:
                step_on(start, 0)
            else:
                lax.fori_loop(start, start + last - first, step_on, 0)
        for plane in range(4):
            hand_over(orders - 1, plane)
        first_row = HALF * (depth + 1)
        count = (ROWS - 2 * first_row) // 8

        def gather(r, carry, depth=depth, first_row=first_row, count=count):
            own_rows = pl.ds(first_row + r, 8, stride=count)
            for step in range(STEPS):
                place = places[depth, step, own_rows, :]
                total = combine(terms, lookup, place, lambda k: pl.ds(HALF - k + r, 8, stride=count), step, orders)
                for plane in range(4):
                    fresh[plane, step, pl.ds(r, 8, stride=count), :] = total[plane]
                picture[depth, step, own_rows, :] = total[0] * total[2] + total[1] * total[3]
            return carry

        lax.fori_loop(0, count, gather, 0)
        for plane in range(4):
            for step in range(STEPS):
                piece = fresh[plane, step, : 8 * count, :]
                if depth == 0:
                    terms[0, plane, step, : 8 * count, :] = piece
                else:
                    centre[plane, step] = piece


def rim_kernel(
    flags, fields, indices0, indices1, above, below, strips0, strips1, inner_picture, table, spread, fresh, image,
    upper, lower, masks, places, picture, result, lookup,
):
    orders = upper.shape[0]
    fill(lookup, table)
    for plane in range(4):
        for step in range(STEPS):
            at = (plane * STEPS + step) * HALO
            upper[0, plane, step, :HALO, :] = above[at : at + HALO, :]
            upper[0, plane, step, HALO:, :] = fields[plane, step, :STRIP, :]
            lower[0, plane, step, :STRIP, :] = fields[plane, step, ROWS - STRIP :, :]
            lower[0, plane, step, STRIP:, :] = below[at : at + HALO, :]
    for step in range(STEPS):
        at = FIELD_ROWS + step * INDEX_HALO
        places[0, 0, step, :INDEX_HALO, :] = above[at : at + INDEX_HALO, :].astype(jnp.int32)
        places[0, 0, step, INDEX_HALO:, :] = indices0[step, :INDEX_HALO, :].astype(jnp.int32)
        places[0, 1, step, :INDEX_HALO, :] = indices0[step, ROWS - INDEX_HALO :, :].astype(jnp.int32)
        places[0, 1, step, INDEX_HALO:, :] = below[at : at + INDEX_HALO, :].astype(jnp.int32)
        places[1, 0, step] = indices1[step, : 2 * INDEX_HALO, :].astype(jnp.int32)
        places[1, 1, step] = indices1[step, ROWS - 2 * INDEX_HALO :, :].astype(jnp.int32)
        masks[step] = column_mask((8, 128), step, flags)
        for depth in range(2):
            picture[depth, step, OFFSET : OFFSET + ROWS, :] = inner_picture[depth, step]

    width = HALO // 8
    sublane = lax.broadcasted_iota(jnp.int32, (8, 128), 0) * width
    for depth in range(2):
        strips = (strips0, strips1)[depth]
        if depth == 1:
            for plane in range(4):
                for step in range(STEPS):
                    upper[0, plane, step, :HALO, :] = fresh[0, plane, step]
                    upper[0, plane, step, HALO:, :] = strips[0, plane, step, :STRIP, :]
                    lower[0, plane, step, :STRIP, :] = strips[0, plane, step, STRIP:, :]
                    lower[0, plane, step, STRIP:, :] = fresh[1, plane, step]

        def step_on(past, carry, first, depth=depth, strips=strips):
            order = 1 if first else past + 2
            shift = order - HALO + HALF * depth
            inside_upper = [jnp.where(sublane + (r + shift) >= 0, 1.0, flags[0]) for r in range(width)]
            inside_lower = [jnp.where(sublane + (r - HALO - shift) < 0, 1.0, flags[1]) for r in range(width)]
            for plane in range(4):
                for step in range(STEPS):
                    upper[order, plane, step, HALO:, :] = strips[order, plane, step, :STRIP, :]
                    lower[order, plane, step, :STRIP, :] = strips[order, plane, step, STRIP:, :]
            for plane in range(4):
                advance(upper, past, plane, 0, 1, width, lambda step, r: inside_upper[r] * masks[step], first)
            for plane in range(4):
                advance(lower, past, plane, STRIP, -1, width, lambda step, r: inside_lower[r] * masks[step], first)
            return carry

        step_on(0, 0, True)
        lax.fori_loop(0, orders - 2, lambda past, carry: step_on(past, carry, False), 0)

        def gather(r, carry, depth=depth):
            for side, terms in enumerate((upper, lower)):
                ahead, start = ((-1, HALF), (1, STRIP - HALF))[side]
                in_places = ((4, 4), (0, 8))[depth][side]
                in_picture = OFFSET + (-HALF + HALF * depth, ROWS - HALF - HALF * depth)[side]
                for step in range(STEPS):
                    place = places[depth, side, step, pl.ds(in_places + r, 8, stride=width), :]
                    total = combine(
                        terms, lookup, place, lambda k: pl.ds(start + ahead * k + r, 8, stride=width), step, orders
                    )
                    for plane in range(4):
                        fresh[side, plane, step, pl.ds(r, 8, stride=width), :] = total[plane]
                    picture[depth, step, pl.ds(in_picture + r, 8, stride=width), :] = total[0] * total[2] + total[1] * total[3]
            return carry

        lax.fori_loop(0, width, gather, 0)

    for step in range(STEPS):
        for depth in range(2):
            piece = picture[depth, step, OFFSET : OFFSET + ROWS, :]
            result[depth * ROWS : (depth + 1) * ROWS, step * 128 : (step + 1) * 128] = piece
    values = move(result[...], spread[: 2 * COLS, :], ((1,), (1,)))
    total = values[:, :COLS] + values[:, COLS:]
    for part in range(8):
        image[part] = total[part * BLOCK : (part + 1) * BLOCK]


def finish_kernel(fresh, centre, spread, source_out, receiver_out, result):
    for plane in range(4):
        for step in range(STEPS):
            rows, cut = plane * ROWS, slice(step * 128, (step + 1) * 128)
            result[rows : rows + HALO, cut] = fresh[0, plane, step]
            result[rows + HALO : rows + ROWS - HALO, cut] = centre[plane, step]
            result[rows + ROWS - HALO : rows + ROWS, cut] = fresh[1, plane, step]
    values = move(result[...], spread[: 2 * COLS, :], ((1,), (1,)))
    for plane in range(4):
        for wave in range(2):
            piece = values[plane * ROWS : (plane + 1) * ROWS, wave * COLS : (wave + 1) * COLS]
            (source_out, receiver_out)[plane // 2][plane % 2, wave] = piece


def full(count):
    return [pl.BlockSpec(memory_space=pltpu.VMEM)] * count


def shape(*dims, dtype=jnp.float32):
    return jax.ShapeDtypeStruct(dims, dtype)


def params(megabytes):
    return pltpu.CompilerParams(vmem_limit_bytes=megabytes * 1024 * 1024)


def cost(flops):
    return pl.CostEstimate(flops=flops, bytes_accessed=2**20, transcendentals=0)


def shift(block, axis, forward):
    count = lax.axis_size(axis)
    pairs = [(i, i + 1) for i in range(count - 1)]
    return lax.ppermute(block, axis, pairs if forward else [(b, a) for a, b in pairs])


def extrapolate(source, receiver, table_index, coef_table):
    orders = coef_table.shape[2]
    at_x, at_y = lax.axis_index("sx"), lax.axis_index("sy")
    flags = jnp.stack(
        [at_x > 0, at_x < lax.axis_size("sx") - 1, at_y > 0, at_y < lax.axis_size("sy") - 1]
    ).astype(jnp.float32)
    table = jnp.transpose(coef_table, (2, 0, 1))
    scalars = [pl.BlockSpec(memory_space=pltpu.SMEM)]

    left, right, waves, places = pl.pallas_call(
        edges_kernel,
        out_shape=(
            pltpu.VMEM((3, ROWS, 128), jnp.float32),
            pltpu.VMEM((3, ROWS, 128), jnp.float32),
            pltpu.VMEM((2, 2, 2, ROWS, COLS), jnp.float32),
            pltpu.VMEM((2, 2, ROWS, COLS), jnp.int32),
        ),
        in_specs=[pl.BlockSpec(memory_space=pltpu.HBM)] * 3,
        out_specs=tuple(full(4)),
        scratch_shapes=[pltpu.SemaphoreType.DMA((3, 4))],
        compiler_params=params(16),
        name="edges",
    )(*(pltpu.with_memory_space_constraint(array, pltpu.HBM) for array in (source, receiver, table_index)))
    low = shift(right, "sy", True)
    high = shift(left, "sy", False)
    own, indices, spread = pl.pallas_call(
        own_kernel,
        out_shape=(shape(4, STEPS, ROWS, 128), shape(2, STEPS, ROWS, 128), shape(WIDE, WIDE, dtype=jnp.bfloat16)),
        in_specs=full(2),
        out_specs=tuple(full(3)),
        scratch_shapes=[pltpu.VMEM((ROWS, 2 * COLS), jnp.float32)],
        compiler_params=params(16),
        cost_estimate=cost(2 * 10**9),
        name="own",
    )(waves, places)
    fields, indices0, top, bottom = pl.pallas_call(
        merge_kernel,
        out_shape=(shape(4, STEPS, ROWS, 128), shape(STEPS, ROWS, 128), shape(SEND, 128), shape(SEND, 128)),
        in_specs=full(5),
        out_specs=tuple(full(4)),
        scratch_shapes=[pltpu.VMEM((5 * ROWS, 128), jnp.float32)],
        compiler_params=params(16),
        name="merge",
    )(own, indices, low, high, spread)
    indices1 = indices[1]
    above = shift(bottom, "sx", True)
    below = shift(top, "sx", False)
    strip = shape(orders, 4, STEPS, 2 * STRIP, 128)
    lookup = pltpu.VMEM((2 * orders, 128), jnp.float32)
    strips0, strips1, picture, centre = pl.pallas_call(
        inner_kernel,
        out_shape=(strip, strip, shape(2, STEPS, ROWS, 128), shape(4, STEPS, ROWS - 2 * HALO, 128)),
        in_specs=scalars + full(4),
        out_specs=tuple(full(4)),
        scratch_shapes=[
            pltpu.VMEM((orders, 4, STEPS, ROWS + 16, 128), jnp.float32),
            pltpu.VMEM((4, STEPS, ROWS - HALO, 128), jnp.float32),
            pltpu.VMEM((STEPS, 8, 128), jnp.float32),
            pltpu.VMEM((2, STEPS, ROWS, 128), jnp.int32),
            lookup,
        ],
        compiler_params=params(32),
        cost_estimate=cost(10**10),
        name="inner",
    )(flags, fields, indices0, indices1, table)
    fresh, image = pl.pallas_call(
        rim_kernel,
        out_shape=(shape(2, 4, STEPS, HALO, 128), shape(8, BLOCK, COLS)),
        in_specs=scalars + full(10),
        out_specs=tuple(full(2)),
        scratch_shapes=[
            pltpu.VMEM((orders, 4, STEPS, HALO + STRIP, 128), jnp.float32),
            pltpu.VMEM((orders, 4, STEPS, HALO + STRIP, 128), jnp.float32),
            pltpu.VMEM((STEPS, 8, 128), jnp.float32),
            pltpu.VMEM((2, 2, STEPS, 2 * INDEX_HALO, 128), jnp.int32),
            pltpu.VMEM((2, STEPS, TALL, 128), jnp.float32),
            pltpu.VMEM((2 * ROWS, WIDE), jnp.float32),
            lookup,
        ],
        compiler_params=params(32),
        name="rim",
    )(flags, fields, indices0, indices1, above, below, strips0, strips1, picture, table, spread)
    source_out, receiver_out = pl.pallas_call(
        finish_kernel,
        out_shape=(shape(2, 2, ROWS, COLS), shape(2, 2, ROWS, COLS)),
        in_specs=full(3),
        out_specs=tuple(full(2)),
        scratch_shapes=[pltpu.VMEM((4 * ROWS, WIDE), jnp.float32)],
        compiler_params=params(16),
        cost_estimate=cost(2 * 10**9),
        name="finish",
    )(fresh, centre, spread)
    return source_out, receiver_out, image


def add_over_freq(pieces, beside):
    groups = [[y * 4 + z * 2 + core for y in range(4) for core in range(2)] for z in range(2)]
    mine = jnp.sum(lax.all_to_all(pieces, "freq", 0, 0, axis_index_groups=groups), axis=0)
    other = lax.ppermute(mine, "freq", [(i, i ^ 2) for i in range(16)])
    other, *beside = lax.optimization_barrier((other, *beside))
    mine = mine + other
    blocks = lax.all_to_all(jnp.broadcast_to(mine[None], pieces.shape), "freq", 0, 0, axis_index_groups=groups)
    return *beside, blocks.reshape(2, ROWS, COLS)


def local(source, receiver, table_index, coef_table):
    source_out, receiver_out, pieces = extrapolate(source, receiver, table_index, coef_table)
    return add_over_freq(pieces, (source_out, receiver_out))


def solution(mesh):
    placed = P(None, "freq", "sx", "sy")
    return jax.shard_map(
        local,
        mesh=mesh,
        in_specs=(placed, placed, placed, P()),
        out_specs=(placed, placed, P(None, "sx", "sy")),
        check_vma=False,
    )
```

```python
import jax
import jax.numpy as jnp
from jax import lax
from jax.experimental import pallas as pl
from jax.experimental.pallas import tpu as pltpu
from jax.sharding import PartitionSpec as P

ROWS, COLS = 64, 256
HALO = 24
HALF = HALO // 2
SIDE = 32
STEPS = 5
INDEX_HALO = 16
FIELD_ROWS = 4 * STEPS * HALO
SEND = FIELD_ROWS + STEPS * INDEX_HALO
WIDE = STEPS * 128
STRIP = 16
OFFSET = 32
TALL = 128
BLOCK = 16


def fill_spread(spread):
    lane = lax.broadcasted_iota(jnp.int32, (128, 128), 1)
    row = lax.broadcasted_iota(jnp.int32, (128, 128), 0)
    for part in range(STEPS):
        if part < 4:
            wave, column = part // 2, SIDE + (part % 2) * 128 + row
        else:
            wave = lax.rem(lax.div(row, SIDE), 2)
            column = lax.rem(row, SIDE) + jnp.where(row < 2 * SIDE, 0, SIDE + COLS)
        goes = wave * 512 + column
        for step in range(STEPS):
            place = lax.div(lane, 64) * 512 + lax.rem(lane, 64) * STEPS + step
            here = jnp.where(goes == place, 1.0, 0.0).astype(jnp.bfloat16)
            spread[part * 128 : (part + 1) * 128, step * 128 : (step + 1) * 128] = here


def dot(left, right, contract):
    return lax.dot_general(left, right, (contract, ((), ())), preferred_element_type=jnp.float32)


def move(left, right, contract):
    high = left.astype(jnp.bfloat16)
    low = (left - high.astype(jnp.float32)).astype(jnp.bfloat16)
    return dot(high, right, contract) + dot(low, right, contract)


def edges_kernel(source, receiver, index, left, right, waves, places, sems):
    copies = [
        [
            pltpu.make_async_copy(field.at[part, wave], waves.at[kind, part, wave], sems.at[kind, 2 * part + wave])
            for part in range(2)
            for wave in range(2)
        ]
        for kind, field in enumerate((source, receiver))
    ]
    copies.append([pltpu.make_async_copy(index.at[depth], places.at[depth], sems.at[2, depth]) for depth in range(2)])
    for copy in sum(copies, []):
        copy.start()
    lane = lax.broadcasted_iota(jnp.int32, (ROWS, 128), 1)

    def join(parts, start):
        total = jnp.zeros((ROWS, 128), jnp.float32)
        for place, part in enumerate(parts):
            shift = (place * SIDE - start) % 128
            moved = part if shift == 0 else pltpu.roll(part, shift, 1)
            total = jnp.where((lane >= place * SIDE) & (lane < (place + 1) * SIDE), moved, total)
        return total

    ends = ((right, 1, 128 - SIDE), (left, 0, 0))
    for kind in range(3):
        for copy in copies[kind]:
            copy.wait()
        for out, tile, start in ends:
            cut = slice(tile * 128, (tile + 1) * 128)
            if kind < 2:
                out[kind] = join([waves[kind, part, wave, :, cut] for part in range(2) for wave in range(2)], start)
            else:
                out[2] = join([places[0, wave, :, cut].astype(jnp.float32) for wave in range(2)], start)


def own_kernel(waves, index, fields, indices, spread, joined):
    fill_spread(spread)
    matrix = spread[: 2 * COLS, :]
    for plane in range(6):
        for wave in range(2):
            cut = slice(wave * COLS, (wave + 1) * COLS)
            if plane < 4:
                joined[:, cut] = waves[plane // 2, plane % 2, wave]
            else:
                joined[:, cut] = index[plane - 4, wave].astype(jnp.float32)
        if plane < 4:
            values = move(joined[...], matrix, ((1,), (0,)))
        else:
            values = dot(joined[...].astype(jnp.bfloat16), matrix, ((1,), (0,)))
        for step in range(STEPS):
            piece = values[:, step * 128 : (step + 1) * 128]
            if plane < 4:
                fields[plane, step] = piece
            else:
                indices[plane - 4, step] = piece


def merge_kernel(own, indices, low, high, spread, fields, indices0, top, bottom, joined):
    lane = lax.broadcasted_iota(jnp.int32, (ROWS, 128), 1)
    matrix = spread[2 * COLS :, :]
    for plane in range(5):
        from_low, from_high = low[plane // 2], high[plane // 2]
        if plane % 2 == 0:
            from_high = pltpu.roll(from_high, 64, 1)
        else:
            from_low = pltpu.roll(from_low, 64, 1)
        joined[plane * ROWS : (plane + 1) * ROWS, :] = jnp.where(lane < 64, from_low, from_high)
    values = move(joined[...], matrix, ((1,), (0,)))
    for plane in range(5):
        for step in range(STEPS):
            piece = values[plane * ROWS : (plane + 1) * ROWS, step * 128 : (step + 1) * 128]
            if plane < 4:
                piece = piece + own[plane, step]
                fields[plane, step] = piece
                rows, at = HALO, (plane * STEPS + step) * HALO
            else:
                piece = piece + indices[0, step]
                indices0[step] = piece
                rows, at = INDEX_HALO, FIELD_ROWS + step * INDEX_HALO
            top[at : at + rows, :] = piece[:rows]
            bottom[at : at + rows, :] = piece[ROWS - rows :]


def advance(terms, past, plane, origin, ahead, count, mask, first):
    now = 0 if first else past + 1

    def rows(first_row):
        return pl.ds(first_row, 8, stride=count)

    def load(r):
        return [terms[now, plane, step, rows(origin + ahead + r), :] for step in range(STEPS)]

    values = [load(r) for r in range(-1, count + 1)]
    pairs = [[a + b for a, b in zip(values[r], values[r + 1])] for r in range(count + 1)]
    for r in range(count):
        column = [a + b for a, b in zip(pairs[r], pairs[r + 1])]
        from_left = pltpu.roll(column[STEPS - 1], 1, 1)
        from_right = pltpu.roll(column[0], 127, 1)
        across = [column[s] + column[s + 1] for s in range(STEPS - 1)]
        both = [(from_left + column[0]) + across[0]]
        both += [across[s - 1] + across[s] for s in range(1, STEPS - 1)]
        both.append(across[STEPS - 2] + (column[STEPS - 1] + from_right))
        for step in range(STEPS):
            moved = mask(step, r) * both[step]
            value = values[r + 1][step]
            if first:
                new = 0.5 * moved - value
            else:
                new = (moved - (value + value)) - terms[past, plane, step, rows(origin + 2 * ahead + r), :]
            terms[now + 1, plane, step, rows(origin + r), :] = new


def combine(terms, table, place, rows, step, orders):
    total = [None] * 4
    for order in range(orders):
        re = jnp.take_along_axis(jnp.broadcast_to(table[order, :][None], (8, 128)), place, axis=1)
        im = jnp.take_along_axis(jnp.broadcast_to(table[orders + order, :][None], (8, 128)), place, axis=1)
        for waves in (0, 2):
            real = terms[order, waves, step, rows(order), :]
            imag = terms[order, waves + 1, step, rows(order), :]
            if waves == 0:
                new = (re * real - im * imag, re * imag + im * real)
            else:
                new = (re * real + im * imag, re * imag - im * real)
            for part in range(2):
                old = total[waves + part]
                total[waves + part] = new[part] if old is None else old + new[part]
    return total


def fill(lookup, table):
    orders, parts, entries = table.shape
    lookup[...] = jnp.zeros(lookup.shape, jnp.float32)
    for order in range(orders):
        for part in range(parts):
            at = part * orders + order
            lookup[at : at + 1, :entries] = table[order, part : part + 1, :]


def column_mask(shape, step, flags):
    column = (lax.broadcasted_iota(jnp.int32, shape, 1) % 64) * STEPS + step
    return 0.25 * jnp.where(column < SIDE, flags[2:3, :], jnp.where(column >= SIDE + COLS, flags[3:4, :], 1.0))


def inner_kernel(
    flags, fields, indices0, indices1, table, strips0, strips1, picture, centre,
    terms, fresh, masks, places, lookup,
):
    orders = terms.shape[0]
    fill(lookup, table)
    for plane in range(4):
        for step in range(STEPS):
            terms[0, plane, step, :ROWS, :] = fields[plane, step]
    for step in range(STEPS):
        places[0, step] = indices0[step].astype(jnp.int32)
        places[1, step] = indices1[step].astype(jnp.int32)
        masks[step] = column_mask((8, 128), step, flags)

    def mask(step, r):
        return masks[step]

    for depth in range(2):
        height = ROWS - 2 * HALF * depth
        strips = (strips0, strips1)[depth]

        def hand_over(order, plane, strips=strips, height=height):
            for step in range(STEPS):
                strips[order, plane, step, :STRIP, :] = terms[order, plane, step, :STRIP, :]
                strips[order, plane, step, STRIP:, :] = terms[order, plane, step, pl.ds(height - STRIP - 2 * order, STRIP), :]

        for first, last in ((0, 1), (1, 3), (3, 7), (7, 11), (11, 12)):
            count = -(-(height - 2 * (first + 1)) // 8)
            count += count == 8

            def step_on(past, carry, first=first, count=count, hand_over=hand_over):
                for plane in range(4):
                    hand_over(0 if first == 0 else past + 1, plane)
                for plane in range(4):
                    advance(terms, past, plane, 0, 1, count, mask, first == 0)
                return carry

            start = max(first - 1, 0)
            if last - first == 1:
                step_on(start, 0)
            else:
                lax.fori_loop(start, start + last - first, step_on, 0)
        for plane in range(4):
            hand_over(orders - 1, plane)
        first_row = HALF * (depth + 1)
        count = (ROWS - 2 * first_row) // 8

        def gather(r, carry, depth=depth, first_row=first_row, count=count):
            own_rows = pl.ds(first_row + r, 8, stride=count)
            for step in range(STEPS):
                place = places[depth, step, own_rows, :]
                total = combine(terms, lookup, place, lambda k: pl.ds(HALF - k + r, 8, stride=count), step, orders)
                for plane in range(4):
                    fresh[plane, step, pl.ds(r, 8, stride=count), :] = total[plane]
                picture[depth, step, own_rows, :] = total[0] * total[2] + total[1] * total[3]
            return carry

        lax.fori_loop(0, count, gather, 0)
        for plane in range(4):
            for step in range(STEPS):
                piece = fresh[plane, step, : 8 * count, :]
                if depth == 0:
                    terms[0, plane, step, : 8 * count, :] = piece
                else:
                    centre[plane, step] = piece


def rim_kernel(
    flags, fields, indices0, indices1, above, below, strips0, strips1, inner_picture, centre, table, spread,
    fresh, image, source_out, receiver_out, upper, lower, masks, places, picture, result, lookup, whole, natural, sems,
):
    orders = upper.shape[0]
    fill(lookup, table)
    for plane in range(4):
        for step in range(STEPS):
            at = (plane * STEPS + step) * HALO
            upper[0, plane, step, :HALO, :] = above[at : at + HALO, :]
            upper[0, plane, step, HALO:, :] = fields[plane, step, :STRIP, :]
            lower[0, plane, step, :STRIP, :] = fields[plane, step, ROWS - STRIP :, :]
            lower[0, plane, step, STRIP:, :] = below[at : at + HALO, :]
    for step in range(STEPS):
        at = FIELD_ROWS + step * INDEX_HALO
        places[0, 0, step, :INDEX_HALO, :] = above[at : at + INDEX_HALO, :].astype(jnp.int32)
        places[0, 0, step, INDEX_HALO:, :] = indices0[step, :INDEX_HALO, :].astype(jnp.int32)
        places[0, 1, step, :INDEX_HALO, :] = indices0[step, ROWS - INDEX_HALO :, :].astype(jnp.int32)
        places[0, 1, step, INDEX_HALO:, :] = below[at : at + INDEX_HALO, :].astype(jnp.int32)
        places[1, 0, step] = indices1[step, : 2 * INDEX_HALO, :].astype(jnp.int32)
        places[1, 1, step] = indices1[step, ROWS - 2 * INDEX_HALO :, :].astype(jnp.int32)
        masks[step] = column_mask((8, 128), step, flags)
        for depth in range(2):
            picture[depth, step, OFFSET : OFFSET + ROWS, :] = inner_picture[depth, step]

    width = HALO // 8
    sublane = lax.broadcasted_iota(jnp.int32, (8, 128), 0) * width
    for depth in range(2):
        strips = (strips0, strips1)[depth]
        if depth == 1:
            for plane in range(4):
                for step in range(STEPS):
                    upper[0, plane, step, :HALO, :] = fresh[0, plane, step]
                    upper[0, plane, step, HALO:, :] = strips[0, plane, step, :STRIP, :]
                    lower[0, plane, step, :STRIP, :] = strips[0, plane, step, STRIP:, :]
                    lower[0, plane, step, STRIP:, :] = fresh[1, plane, step]

        def step_on(past, carry, first, depth=depth, strips=strips):
            order = 1 if first else past + 2
            shift = order - HALO + HALF * depth
            inside_upper = [jnp.where(sublane + (r + shift) >= 0, 1.0, flags[0:1, :]) for r in range(width)]
            inside_lower = [jnp.where(sublane + (r - HALO - shift) < 0, 1.0, flags[1:2, :]) for r in range(width)]
            for plane in range(4):
                for step in range(STEPS):
                    upper[order, plane, step, HALO:, :] = strips[order, plane, step, :STRIP, :]
                    lower[order, plane, step, :STRIP, :] = strips[order, plane, step, STRIP:, :]
            for plane in range(4):
                advance(upper, past, plane, 0, 1, width, lambda step, r: inside_upper[r] * masks[step], first)
            for plane in range(4):
                advance(lower, past, plane, STRIP, -1, width, lambda step, r: inside_lower[r] * masks[step], first)
            return carry

        step_on(0, 0, True)
        lax.fori_loop(0, orders - 2, lambda past, carry: step_on(past, carry, False), 0)

        def gather(r, carry, depth=depth):
            for side, terms in enumerate((upper, lower)):
                ahead, start = ((-1, HALF), (1, STRIP - HALF))[side]
                in_places = ((4, 4), (0, 8))[depth][side]
                in_picture = OFFSET + (-HALF + HALF * depth, ROWS - HALF - HALF * depth)[side]
                for step in range(STEPS):
                    place = places[depth, side, step, pl.ds(in_places + r, 8, stride=width), :]
                    total = combine(
                        terms, lookup, place, lambda k: pl.ds(start + ahead * k + r, 8, stride=width), step, orders
                    )
                    for plane in range(4):
                        fresh[side, plane, step, pl.ds(r, 8, stride=width), :] = total[plane]
                    picture[depth, step, pl.ds(in_picture + r, 8, stride=width), :] = total[0] * total[2] + total[1] * total[3]
            return carry

        lax.fori_loop(0, width, gather, 0)

    for step in range(STEPS):
        for depth in range(2):
            piece = picture[depth, step, OFFSET : OFFSET + ROWS, :]
            result[depth * ROWS : (depth + 1) * ROWS, step * 128 : (step + 1) * 128] = piece
    values = move(result[...], spread[: 2 * COLS, :], ((1,), (1,)))
    total = values[:, :COLS] + values[:, COLS:]
    for part in range(8):
        image[part] = total[part * BLOCK : (part + 1) * BLOCK]


    @pl.when(flags[4, 0] > 0.5)
    def _():
        to_natural(fresh, centre, spread, source_out, receiver_out, whole, natural, sems)


def to_natural(fresh, centre, spread, source_out, receiver_out, whole, natural, sems):
    for plane in range(4):
        for step in range(STEPS):
            rows, cut = plane * ROWS, slice(step * 128, (step + 1) * 128)
            whole[rows : rows + HALO, cut] = fresh[0, plane, step]
            whole[rows + HALO : rows + ROWS - HALO, cut] = centre[plane, step]
            whole[rows + ROWS - HALO : rows + ROWS, cut] = fresh[1, plane, step]
    values = move(whole[...], spread[: 2 * COLS, :], ((1,), (1,)))
    for plane in range(4):
        for wave in range(2):
            piece = values[plane * ROWS : (plane + 1) * ROWS, wave * COLS : (wave + 1) * COLS]
            natural[plane // 2, plane % 2, wave] = piece
    copies = [pltpu.make_async_copy(natural.at[kind], out, sems.at[kind]) for kind, out in enumerate((source_out, receiver_out))]
    for copy in copies:
        copy.start()
    for copy in copies:
        copy.wait()


def finish_kernel(flags, fresh, centre, spread, source_in, receiver_in, source_out, receiver_out, whole, natural, sems):
    del source_in, receiver_in

    @pl.when(flags[4, 0] < 0.5)
    def _():
        to_natural(fresh, centre, spread, source_out, receiver_out, whole, natural, sems)


def full(count):
    return [pl.BlockSpec(memory_space=pltpu.VMEM)] * count


def shape(*dims, dtype=jnp.float32):
    return jax.ShapeDtypeStruct(dims, dtype)


def params(megabytes):
    return pltpu.CompilerParams(vmem_limit_bytes=megabytes * 1024 * 1024)


def cost(flops):
    return pl.CostEstimate(flops=flops, bytes_accessed=2**20, transcendentals=0)


def shift(block, axis, forward):
    count = lax.axis_size(axis)
    pairs = [(i, i + 1) for i in range(count - 1)]
    return lax.ppermute(block, axis, pairs if forward else [(b, a) for a, b in pairs])


def extrapolate(source, receiver, table_index, coef_table):
    orders = coef_table.shape[2]
    at_x, at_y = lax.axis_index("sx"), lax.axis_index("sy")
    early = (lax.axis_index("freq") // 2) % 2 == 0
    row = lax.broadcasted_iota(jnp.int32, (8, 128), 0)
    flags = jnp.zeros((8, 128), jnp.float32)
    tests = [at_x > 0, at_x < lax.axis_size("sx") - 1, at_y > 0, at_y < lax.axis_size("sy") - 1, early]
    for place, test in enumerate(tests):
        flags = jnp.where((row == place) & test, 1.0, flags)
    table = jnp.transpose(coef_table, (2, 0, 1))

    left, right, waves, places = pl.pallas_call(
        edges_kernel,
        out_shape=(
            pltpu.VMEM((3, ROWS, 128), jnp.float32),
            pltpu.VMEM((3, ROWS, 128), jnp.float32),
            pltpu.VMEM((2, 2, 2, ROWS, COLS), jnp.float32),
            pltpu.VMEM((2, 2, ROWS, COLS), jnp.int32),
        ),
        in_specs=[pl.BlockSpec(memory_space=pltpu.HBM)] * 3,
        out_specs=tuple(full(4)),
        scratch_shapes=[pltpu.SemaphoreType.DMA((3, 4))],
        compiler_params=params(16),
        name="edges",
    )(*(pltpu.with_memory_space_constraint(array, pltpu.HBM) for array in (source, receiver, table_index)))
    low = shift(right, "sy", True)
    high = shift(left, "sy", False)
    own, indices, spread = pl.pallas_call(
        own_kernel,
        out_shape=(shape(4, STEPS, ROWS, 128), shape(2, STEPS, ROWS, 128), shape(WIDE, WIDE, dtype=jnp.bfloat16)),
        in_specs=full(2),
        out_specs=tuple(full(3)),
        scratch_shapes=[pltpu.VMEM((ROWS, 2 * COLS), jnp.float32)],
        compiler_params=params(16),
        cost_estimate=cost(2 * 10**9),
        name="own",
    )(waves, places)
    fields, indices0, top, bottom = pl.pallas_call(
        merge_kernel,
        out_shape=(shape(4, STEPS, ROWS, 128), shape(STEPS, ROWS, 128), shape(SEND, 128), shape(SEND, 128)),
        in_specs=full(5),
        out_specs=tuple(full(4)),
        scratch_shapes=[pltpu.VMEM((5 * ROWS, 128), jnp.float32)],
        compiler_params=params(16),
        name="merge",
    )(own, indices, low, high, spread)
    indices1 = indices[1]
    above = shift(bottom, "sx", True)
    below = shift(top, "sx", False)
    strip = shape(orders, 4, STEPS, 2 * STRIP, 128)
    lookup = pltpu.VMEM((2 * orders, 128), jnp.float32)
    strips0, strips1, picture, centre = pl.pallas_call(
        inner_kernel,
        out_shape=(strip, strip, shape(2, STEPS, ROWS, 128), shape(4, STEPS, ROWS - 2 * HALO, 128)),
        in_specs=full(5),
        out_specs=tuple(full(4)),
        scratch_shapes=[
            pltpu.VMEM((orders, 4, STEPS, ROWS + 16, 128), jnp.float32),
            pltpu.VMEM((4, STEPS, ROWS - HALO, 128), jnp.float32),
            pltpu.VMEM((STEPS, 8, 128), jnp.float32),
            pltpu.VMEM((2, STEPS, ROWS, 128), jnp.int32),
            lookup,
        ],
        compiler_params=params(32),
        cost_estimate=cost(10**10),
        name="inner",
    )(flags, fields, indices0, indices1, table)
    back = [
        pltpu.VMEM((4 * ROWS, WIDE), jnp.float32),
        pltpu.VMEM((2, 2, 2, ROWS, COLS), jnp.float32),
        pltpu.SemaphoreType.DMA((2,)),
    ]
    hbm = [pl.BlockSpec(memory_space=pltpu.HBM)] * 2
    fresh, image, source_out, receiver_out = pl.pallas_call(
        rim_kernel,
        out_shape=(
            shape(2, 4, STEPS, HALO, 128),
            shape(8, BLOCK, COLS),
            shape(2, 2, ROWS, COLS),
            shape(2, 2, ROWS, COLS),
        ),
        in_specs=full(12),
        out_specs=tuple(full(2) + hbm),
        scratch_shapes=[
            pltpu.VMEM((orders, 4, STEPS, HALO + STRIP, 128), jnp.float32),
            pltpu.VMEM((orders, 4, STEPS, HALO + STRIP, 128), jnp.float32),
            pltpu.VMEM((STEPS, 8, 128), jnp.float32),
            pltpu.VMEM((2, 2, STEPS, 2 * INDEX_HALO, 128), jnp.int32),
            pltpu.VMEM((2, STEPS, TALL, 128), jnp.float32),
            pltpu.VMEM((2 * ROWS, WIDE), jnp.float32),
            lookup,
            *back,
        ],
        compiler_params=params(32),
        name="rim",
    )(flags, fields, indices0, indices1, above, below, strips0, strips1, picture, centre, table, spread)
    source_out, receiver_out = pl.pallas_call(
        finish_kernel,
        out_shape=(shape(2, 2, ROWS, COLS), shape(2, 2, ROWS, COLS)),
        in_specs=full(4) + hbm,
        out_specs=tuple(hbm),
        scratch_shapes=back,
        input_output_aliases={4: 0, 5: 1},
        compiler_params=params(16),
        cost_estimate=cost(2 * 10**9),
        name="finish",
    )(flags, fresh, centre, spread, source_out, receiver_out)
    return source_out, receiver_out, image


def add_over_freq(pieces, beside):
    groups = [[y * 4 + z * 2 + core for y in range(4) for core in range(2)] for z in range(2)]
    mine = jnp.sum(lax.all_to_all(pieces, "freq", 0, 0, axis_index_groups=groups), axis=0)
    other = lax.ppermute(mine, "freq", [(i, i ^ 2) for i in range(16)])
    other, *beside = lax.optimization_barrier((other, *beside))
    mine = mine + other
    blocks = lax.all_to_all(jnp.broadcast_to(mine[None], pieces.shape), "freq", 0, 0, axis_index_groups=groups)
    return *beside, blocks.reshape(2, ROWS, COLS)


def local(source, receiver, table_index, coef_table):
    source_out, receiver_out, pieces = extrapolate(source, receiver, table_index, coef_table)
    return add_over_freq(pieces, (source_out, receiver_out))


def solution(mesh):
    placed = P(None, "freq", "sx", "sy")
    return jax.shard_map(
        local,
        mesh=mesh,
        in_specs=(placed, placed, placed, P()),
        out_specs=(placed, placed, P(None, "sx", "sy")),
        check_vma=False,
    )
```

```python
import jax
import jax.numpy as jnp
from jax import lax
from jax.experimental import pallas as pl
from jax.experimental.pallas import tpu as pltpu
from jax.sharding import PartitionSpec as P

ROWS, COLS = 64, 256
HALO = 24
HALF = HALO // 2
SIDE = 32
STEPS = 5
INDEX_HALO = 16
FIELD_ROWS = 4 * STEPS * HALO
SEND = FIELD_ROWS + STEPS * INDEX_HALO
WIDE = STEPS * 128
STRIP = 16
OFFSET = 32
TALL = 128
BLOCK = 16


def fill_spread(spread):
    lane = lax.broadcasted_iota(jnp.int32, (128, 128), 1)
    row = lax.broadcasted_iota(jnp.int32, (128, 128), 0)
    for part in range(STEPS):
        if part < 4:
            wave, column = part // 2, SIDE + (part % 2) * 128 + row
        else:
            wave = lax.rem(lax.div(row, SIDE), 2)
            column = lax.rem(row, SIDE) + jnp.where(row < 2 * SIDE, 0, SIDE + COLS)
        goes = wave * 512 + column
        for step in range(STEPS):
            place = lax.div(lane, 64) * 512 + lax.rem(lane, 64) * STEPS + step
            here = jnp.where(goes == place, 1.0, 0.0).astype(jnp.bfloat16)
            spread[part * 128 : (part + 1) * 128, step * 128 : (step + 1) * 128] = here


def dot(left, right, contract):
    return lax.dot_general(left, right, (contract, ((), ())), preferred_element_type=jnp.float32)


def move(left, right, contract):
    high = left.astype(jnp.bfloat16)
    low = (left - high.astype(jnp.float32)).astype(jnp.bfloat16)
    return dot(high, right, contract) + dot(low, right, contract)


def edges_kernel(source, receiver, index, left, right, waves, places, sems):
    copies = [
        [
            pltpu.make_async_copy(field.at[part, wave], waves.at[kind, part, wave], sems.at[kind, 2 * part + wave])
            for part in range(2)
            for wave in range(2)
        ]
        for kind, field in enumerate((source, receiver))
    ]
    copies.append([pltpu.make_async_copy(index.at[depth], places.at[depth], sems.at[2, depth]) for depth in range(2)])
    for copy in sum(copies, []):
        copy.start()
    lane = lax.broadcasted_iota(jnp.int32, (ROWS, 128), 1)

    def join(parts, start):
        total = jnp.zeros((ROWS, 128), jnp.float32)
        for place, part in enumerate(parts):
            shift = (place * SIDE - start) % 128
            moved = part if shift == 0 else pltpu.roll(part, shift, 1)
            total = jnp.where((lane >= place * SIDE) & (lane < (place + 1) * SIDE), moved, total)
        return total

    ends = ((right, 1, 128 - SIDE), (left, 0, 0))
    for kind in range(3):
        for copy in copies[kind]:
            copy.wait()
        for out, tile, start in ends:
            cut = slice(tile * 128, (tile + 1) * 128)
            if kind < 2:
                out[kind] = join([waves[kind, part, wave, :, cut] for part in range(2) for wave in range(2)], start)
            else:
                out[2] = join([places[0, wave, :, cut].astype(jnp.float32) for wave in range(2)], start)


def own_kernel(waves, index, fields, indices, spread, joined):
    fill_spread(spread)
    matrix = spread[: 2 * COLS, :]
    for plane in range(6):
        for wave in range(2):
            cut = slice(wave * COLS, (wave + 1) * COLS)
            if plane < 4:
                joined[:, cut] = waves[plane // 2, plane % 2, wave]
            else:
                joined[:, cut] = index[plane - 4, wave].astype(jnp.float32)
        if plane < 4:
            values = move(joined[...], matrix, ((1,), (0,)))
        else:
            values = dot(joined[...].astype(jnp.bfloat16), matrix, ((1,), (0,)))
        for step in range(STEPS):
            piece = values[:, step * 128 : (step + 1) * 128]
            if plane < 4:
                fields[plane, step] = piece
            else:
                indices[plane - 4, step] = piece


def merge_kernel(own, indices, low, high, spread, fields, indices0, top, bottom, joined):
    lane = lax.broadcasted_iota(jnp.int32, (ROWS, 128), 1)
    matrix = spread[2 * COLS :, :]
    for plane in range(5):
        from_low, from_high = low[plane // 2], high[plane // 2]
        if plane % 2 == 0:
            from_high = pltpu.roll(from_high, 64, 1)
        else:
            from_low = pltpu.roll(from_low, 64, 1)
        joined[plane * ROWS : (plane + 1) * ROWS, :] = jnp.where(lane < 64, from_low, from_high)
    values = move(joined[...], matrix, ((1,), (0,)))
    for plane in range(5):
        for step in range(STEPS):
            piece = values[plane * ROWS : (plane + 1) * ROWS, step * 128 : (step + 1) * 128]
            if plane < 4:
                piece = piece + own[plane, step]
                fields[plane, step] = piece
                rows, at = HALO, (plane * STEPS + step) * HALO
            else:
                piece = piece + indices[0, step]
                indices0[step] = piece
                rows, at = INDEX_HALO, FIELD_ROWS + step * INDEX_HALO
            top[at : at + rows, :] = piece[:rows]
            bottom[at : at + rows, :] = piece[ROWS - rows :]


def advance(terms, past, plane, origin, ahead, count, mask, first):
    now = 0 if first else past + 1

    def rows(first_row):
        return pl.ds(first_row, 8, stride=count)

    def load(r):
        return [terms[now, plane, step, rows(origin + ahead + r), :] for step in range(STEPS)]

    values = [load(r) for r in range(-1, count + 1)]
    pairs = [[a + b for a, b in zip(values[r], values[r + 1])] for r in range(count + 1)]
    for r in range(count):
        column = [a + b for a, b in zip(pairs[r], pairs[r + 1])]
        from_left = pltpu.roll(column[STEPS - 1], 1, 1)
        from_right = pltpu.roll(column[0], 127, 1)
        across = [column[s] + column[s + 1] for s in range(STEPS - 1)]
        both = [(from_left + column[0]) + across[0]]
        both += [across[s - 1] + across[s] for s in range(1, STEPS - 1)]
        both.append(across[STEPS - 2] + (column[STEPS - 1] + from_right))
        for step in range(STEPS):
            moved = mask(step, r) * both[step]
            value = values[r + 1][step]
            if first:
                new = 0.5 * moved - value
            else:
                new = (moved - (value + value)) - terms[past, plane, step, rows(origin + 2 * ahead + r), :]
            terms[now + 1, plane, step, rows(origin + r), :] = new


def combine(terms, table, place, rows, step, orders):
    total = [None] * 4
    for order in range(orders):
        re = jnp.take_along_axis(jnp.broadcast_to(table[order, :][None], (8, 128)), place, axis=1)
        im = jnp.take_along_axis(jnp.broadcast_to(table[orders + order, :][None], (8, 128)), place, axis=1)
        for waves in (0, 2):
            real = terms[order, waves, step, rows(order), :]
            imag = terms[order, waves + 1, step, rows(order), :]
            if waves == 0:
                new = (re * real - im * imag, re * imag + im * real)
            else:
                new = (re * real + im * imag, re * imag - im * real)
            for part in range(2):
                old = total[waves + part]
                total[waves + part] = new[part] if old is None else old + new[part]
    return total


def fill(lookup, table):
    orders, parts, entries = table.shape
    lookup[...] = jnp.zeros(lookup.shape, jnp.float32)
    for order in range(orders):
        for part in range(parts):
            at = part * orders + order
            lookup[at : at + 1, :entries] = table[order, part : part + 1, :]


def column_mask(shape, step, flags):
    column = (lax.broadcasted_iota(jnp.int32, shape, 1) % 64) * STEPS + step
    return 0.25 * jnp.where(column < SIDE, flags[2:3, :], jnp.where(column >= SIDE + COLS, flags[3:4, :], 1.0))


def inner_kernel(
    flags, fields, indices0, indices1, table, strips0, strips1, picture, centre,
    terms, fresh, masks, places, lookup,
):
    orders = terms.shape[0]
    fill(lookup, table)
    for plane in range(4):
        for step in range(STEPS):
            terms[0, plane, step, :ROWS, :] = fields[plane, step]
    for step in range(STEPS):
        places[0, step] = indices0[step].astype(jnp.int32)
        places[1, step] = indices1[step].astype(jnp.int32)
        masks[step] = column_mask((8, 128), step, flags)

    def mask(step, r):
        return masks[step]

    for depth in range(2):
        height = ROWS - 2 * HALF * depth
        strips = (strips0, strips1)[depth]

        def hand_over(order, plane, strips=strips, height=height):
            for step in range(STEPS):
                strips[order, plane, step, :STRIP, :] = terms[order, plane, step, :STRIP, :]
                strips[order, plane, step, STRIP:, :] = terms[order, plane, step, pl.ds(height - STRIP - 2 * order, STRIP), :]

        for first, last in ((0, 1), (1, 3), (3, 7), (7, 11), (11, 12)):
            count = -(-(height - 2 * (first + 1)) // 8)
            count += count == 8

            def step_on(past, carry, first=first, count=count, hand_over=hand_over):
                for plane in range(4):
                    hand_over(0 if first == 0 else past + 1, plane)
                for plane in range(4):
                    advance(terms, past, plane, 0, 1, count, mask, first == 0)
                return carry

            start = max(first - 1, 0)
            if last - first == 1:
                step_on(start, 0)
            else:
                lax.fori_loop(start, start + last - first, step_on, 0)
        for plane in range(4):
            hand_over(orders - 1, plane)
        first_row = HALF * (depth + 1)
        count = (ROWS - 2 * first_row) // 8

        def gather(r, carry, depth=depth, first_row=first_row, count=count):
            own_rows = pl.ds(first_row + r, 8, stride=count)
            for step in range(STEPS):
                place = places[depth, step, own_rows, :]
                total = combine(terms, lookup, place, lambda k: pl.ds(HALF - k + r, 8, stride=count), step, orders)
                for plane in range(4):
                    fresh[plane, step, pl.ds(r, 8, stride=count), :] = total[plane]
                picture[depth, step, own_rows, :] = total[0] * total[2] + total[1] * total[3]
            return carry

        lax.fori_loop(0, count, gather, 0)
        for plane in range(4):
            for step in range(STEPS):
                piece = fresh[plane, step, : 8 * count, :]
                if depth == 0:
                    terms[0, plane, step, : 8 * count, :] = piece
                else:
                    centre[plane, step] = piece


def rim_kernel(
    flags, fields, indices0, indices1, above, below, strips0, strips1, inner_picture, table, spread, fresh, image,
    upper, lower, masks, places, picture, result, lookup,
):
    orders = upper.shape[0]
    fill(lookup, table)
    for plane in range(4):
        for step in range(STEPS):
            at = (plane * STEPS + step) * HALO
            upper[0, plane, step, :HALO, :] = above[at : at + HALO, :]
            upper[0, plane, step, HALO:, :] = fields[plane, step, :STRIP, :]
            lower[0, plane, step, :STRIP, :] = fields[plane, step, ROWS - STRIP :, :]
            lower[0, plane, step, STRIP:, :] = below[at : at + HALO, :]
    for step in range(STEPS):
        at = FIELD_ROWS + step * INDEX_HALO
        places[0, 0, step, :INDEX_HALO, :] = above[at : at + INDEX_HALO, :].astype(jnp.int32)
        places[0, 0, step, INDEX_HALO:, :] = indices0[step, :INDEX_HALO, :].astype(jnp.int32)
        places[0, 1, step, :INDEX_HALO, :] = indices0[step, ROWS - INDEX_HALO :, :].astype(jnp.int32)
        places[0, 1, step, INDEX_HALO:, :] = below[at : at + INDEX_HALO, :].astype(jnp.int32)
        places[1, 0, step] = indices1[step, : 2 * INDEX_HALO, :].astype(jnp.int32)
        places[1, 1, step] = indices1[step, ROWS - 2 * INDEX_HALO :, :].astype(jnp.int32)
        masks[step] = column_mask((8, 128), step, flags)
        for depth in range(2):
            picture[depth, step, OFFSET : OFFSET + ROWS, :] = inner_picture[depth, step]

    width = HALO // 8
    sublane = lax.broadcasted_iota(jnp.int32, (8, 128), 0) * width
    for depth in range(2):
        strips = (strips0, strips1)[depth]
        if depth == 1:
            for plane in range(4):
                for step in range(STEPS):
                    upper[0, plane, step, :HALO, :] = fresh[0, plane, step]
                    upper[0, plane, step, HALO:, :] = strips[0, plane, step, :STRIP, :]
                    lower[0, plane, step, :STRIP, :] = strips[0, plane, step, STRIP:, :]
                    lower[0, plane, step, STRIP:, :] = fresh[1, plane, step]

        def step_on(past, carry, first, depth=depth, strips=strips):
            order = 1 if first else past + 2
            shift = order - HALO + HALF * depth
            inside_upper = [jnp.where(sublane + (r + shift) >= 0, 1.0, flags[0:1, :]) for r in range(width)]
            inside_lower = [jnp.where(sublane + (r - HALO - shift) < 0, 1.0, flags[1:2, :]) for r in range(width)]
            for plane in range(4):
                for step in range(STEPS):
                    upper[order, plane, step, HALO:, :] = strips[order, plane, step, :STRIP, :]
                    lower[order, plane, step, :STRIP, :] = strips[order, plane, step, STRIP:, :]
            for plane in range(4):
                advance(upper, past, plane, 0, 1, width, lambda step, r: inside_upper[r] * masks[step], first)
            for plane in range(4):
                advance(lower, past, plane, STRIP, -1, width, lambda step, r: inside_lower[r] * masks[step], first)
            return carry

        step_on(0, 0, True)
        lax.fori_loop(0, orders - 2, lambda past, carry: step_on(past, carry, False), 0)

        def gather(r, carry, depth=depth):
            for side, terms in enumerate((upper, lower)):
                ahead, start = ((-1, HALF), (1, STRIP - HALF))[side]
                in_places = ((4, 4), (0, 8))[depth][side]
                in_picture = OFFSET + (-HALF + HALF * depth, ROWS - HALF - HALF * depth)[side]
                for step in range(STEPS):
                    place = places[depth, side, step, pl.ds(in_places + r, 8, stride=width), :]
                    total = combine(
                        terms, lookup, place, lambda k: pl.ds(start + ahead * k + r, 8, stride=width), step, orders
                    )
                    for plane in range(4):
                        fresh[side, plane, step, pl.ds(r, 8, stride=width), :] = total[plane]
                    picture[depth, step, pl.ds(in_picture + r, 8, stride=width), :] = total[0] * total[2] + total[1] * total[3]
            return carry

        lax.fori_loop(0, width, gather, 0)

    for step in range(STEPS):
        for depth in range(2):
            piece = picture[depth, step, OFFSET : OFFSET + ROWS, :]
            result[depth * ROWS : (depth + 1) * ROWS, step * 128 : (step + 1) * 128] = piece
    values = move(result[...], spread[: 2 * COLS, :], ((1,), (1,)))
    total = values[:, :COLS] + values[:, COLS:]
    for part in range(8):
        image[part] = total[part * BLOCK : (part + 1) * BLOCK]


def finish_kernel(fresh, centre, spread, source_out, receiver_out, result):
    for plane in range(4):
        for step in range(STEPS):
            rows, cut = plane * ROWS, slice(step * 128, (step + 1) * 128)
            result[rows : rows + HALO, cut] = fresh[0, plane, step]
            result[rows + HALO : rows + ROWS - HALO, cut] = centre[plane, step]
            result[rows + ROWS - HALO : rows + ROWS, cut] = fresh[1, plane, step]
    values = move(result[...], spread[: 2 * COLS, :], ((1,), (1,)))
    for plane in range(4):
        for wave in range(2):
            piece = values[plane * ROWS : (plane + 1) * ROWS, wave * COLS : (wave + 1) * COLS]
            (source_out, receiver_out)[plane // 2][plane % 2, wave] = piece


def full(count):
    return [pl.BlockSpec(memory_space=pltpu.VMEM)] * count


def shape(*dims, dtype=jnp.float32):
    return jax.ShapeDtypeStruct(dims, dtype)


def params(megabytes):
    return pltpu.CompilerParams(vmem_limit_bytes=megabytes * 1024 * 1024)


def cost(flops):
    return pl.CostEstimate(flops=flops, bytes_accessed=2**20, transcendentals=0)


def shift(block, axis, forward):
    count = lax.axis_size(axis)
    pairs = [(i, i + 1) for i in range(count - 1)]
    return lax.ppermute(block, axis, pairs if forward else [(b, a) for a, b in pairs])


def extrapolate(source, receiver, table_index, coef_table):
    orders = coef_table.shape[2]
    at_x, at_y = lax.axis_index("sx"), lax.axis_index("sy")
    row = lax.broadcasted_iota(jnp.int32, (8, 128), 0)
    flags = jnp.zeros((8, 128), jnp.float32)
    tests = [at_x > 0, at_x < lax.axis_size("sx") - 1, at_y > 0, at_y < lax.axis_size("sy") - 1]
    for place, test in enumerate(tests):
        flags = jnp.where((row == place) & test, 1.0, flags)
    table = jnp.transpose(coef_table, (2, 0, 1))

    left, right, waves, places = pl.pallas_call(
        edges_kernel,
        out_shape=(
            pltpu.VMEM((3, ROWS, 128), jnp.float32),
            pltpu.VMEM((3, ROWS, 128), jnp.float32),
            pltpu.VMEM((2, 2, 2, ROWS, COLS), jnp.float32),
            pltpu.VMEM((2, 2, ROWS, COLS), jnp.int32),
        ),
        in_specs=[pl.BlockSpec(memory_space=pltpu.HBM)] * 3,
        out_specs=tuple(full(4)),
        scratch_shapes=[pltpu.SemaphoreType.DMA((3, 4))],
        compiler_params=params(16),
        name="edges",
    )(*(pltpu.with_memory_space_constraint(array, pltpu.HBM) for array in (source, receiver, table_index)))
    low = shift(right, "sy", True)
    high = shift(left, "sy", False)
    own, indices, spread = pl.pallas_call(
        own_kernel,
        out_shape=(shape(4, STEPS, ROWS, 128), shape(2, STEPS, ROWS, 128), shape(WIDE, WIDE, dtype=jnp.bfloat16)),
        in_specs=full(2),
        out_specs=tuple(full(3)),
        scratch_shapes=[pltpu.VMEM((ROWS, 2 * COLS), jnp.float32)],
        compiler_params=params(16),
        cost_estimate=cost(2 * 10**9),
        name="own",
    )(waves, places)
    fields, indices0, top, bottom = pl.pallas_call(
        merge_kernel,
        out_shape=(shape(4, STEPS, ROWS, 128), shape(STEPS, ROWS, 128), shape(SEND, 128), shape(SEND, 128)),
        in_specs=full(5),
        out_specs=tuple(full(4)),
        scratch_shapes=[pltpu.VMEM((5 * ROWS, 128), jnp.float32)],
        compiler_params=params(16),
        name="merge",
    )(own, indices, low, high, spread)
    indices1 = indices[1]
    above = shift(bottom, "sx", True)
    below = shift(top, "sx", False)
    strip = shape(orders, 4, STEPS, 2 * STRIP, 128)
    lookup = pltpu.VMEM((2 * orders, 128), jnp.float32)
    strips0, strips1, picture, centre = pl.pallas_call(
        inner_kernel,
        out_shape=(strip, strip, shape(2, STEPS, ROWS, 128), shape(4, STEPS, ROWS - 2 * HALO, 128)),
        in_specs=full(5),
        out_specs=tuple(full(4)),
        scratch_shapes=[
            pltpu.VMEM((orders, 4, STEPS, ROWS + 16, 128), jnp.float32),
            pltpu.VMEM((4, STEPS, ROWS - HALO, 128), jnp.float32),
            pltpu.VMEM((STEPS, 8, 128), jnp.float32),
            pltpu.VMEM((2, STEPS, ROWS, 128), jnp.int32),
            lookup,
        ],
        compiler_params=params(32),
        cost_estimate=cost(10**10),
        name="inner",
    )(flags, fields, indices0, indices1, table)
    fresh, image = pl.pallas_call(
        rim_kernel,
        out_shape=(shape(2, 4, STEPS, HALO, 128), shape(8, BLOCK, COLS)),
        in_specs=full(11),
        out_specs=tuple(full(2)),
        scratch_shapes=[
            pltpu.VMEM((orders, 4, STEPS, HALO + STRIP, 128), jnp.float32),
            pltpu.VMEM((orders, 4, STEPS, HALO + STRIP, 128), jnp.float32),
            pltpu.VMEM((STEPS, 8, 128), jnp.float32),
            pltpu.VMEM((2, 2, STEPS, 2 * INDEX_HALO, 128), jnp.int32),
            pltpu.VMEM((2, STEPS, TALL, 128), jnp.float32),
            pltpu.VMEM((2 * ROWS, WIDE), jnp.float32),
            lookup,
        ],
        compiler_params=params(32),
        name="rim",
    )(flags, fields, indices0, indices1, above, below, strips0, strips1, picture, table, spread)
    source_out, receiver_out = pl.pallas_call(
        finish_kernel,
        out_shape=(shape(2, 2, ROWS, COLS), shape(2, 2, ROWS, COLS)),
        in_specs=full(3),
        out_specs=tuple(full(2)),
        scratch_shapes=[pltpu.VMEM((4 * ROWS, WIDE), jnp.float32)],
        compiler_params=params(16),
        cost_estimate=cost(2 * 10**9),
        name="finish",
    )(fresh, centre, spread)
    return source_out, receiver_out, image


def add_over_freq(pieces, beside):
    groups = [[y * 4 + z * 2 + core for y in range(4) for core in range(2)] for z in range(2)]
    mine = jnp.sum(lax.all_to_all(pieces, "freq", 0, 0, axis_index_groups=groups), axis=0)
    other = lax.ppermute(mine, "freq", [(i, i ^ 2) for i in range(16)])
    other, *beside = lax.optimization_barrier((other, *beside))
    mine = mine + other
    blocks = lax.all_to_all(jnp.broadcast_to(mine[None], pieces.shape), "freq", 0, 0, axis_index_groups=groups)
    return *beside, blocks.reshape(2, ROWS, COLS)


def local(source, receiver, table_index, coef_table):
    source_out, receiver_out, pieces = extrapolate(source, receiver, table_index, coef_table)
    return add_over_freq(pieces, (source_out, receiver_out))


def solution(mesh):
    placed = P(None, "freq", "sx", "sy")
    return jax.shard_map(
        local,
        mesh=mesh,
        in_specs=(placed, placed, placed, P()),
        out_specs=(placed, placed, P(None, "sx", "sy")),
        check_vma=False,
    )
```

```python
import jax
import jax.numpy as jnp
from jax import lax
from jax.experimental import pallas as pl
from jax.experimental.pallas import tpu as pltpu
from jax.sharding import PartitionSpec as P

ROWS, COLS = 64, 256
HALO = 24
HALF = HALO // 2
SIDE = 32
STEPS = 5
INDEX_HALO = 16
FIELD_ROWS = 4 * STEPS * HALO
SEND = FIELD_ROWS + STEPS * INDEX_HALO
WIDE = STEPS * 128
STRIP = 16
OFFSET = 32
TALL = 128
BLOCK = 16


def fill_spread(spread):
    lane = lax.broadcasted_iota(jnp.int32, (128, 128), 1)
    row = lax.broadcasted_iota(jnp.int32, (128, 128), 0)
    for part in range(STEPS):
        if part < 4:
            wave, column = part // 2, SIDE + (part % 2) * 128 + row
        else:
            wave = lax.rem(lax.div(row, SIDE), 2)
            column = lax.rem(row, SIDE) + jnp.where(row < 2 * SIDE, 0, SIDE + COLS)
        goes = wave * 512 + column
        for step in range(STEPS):
            place = lax.div(lane, 64) * 512 + lax.rem(lane, 64) * STEPS + step
            here = jnp.where(goes == place, 1.0, 0.0).astype(jnp.bfloat16)
            spread[part * 128 : (part + 1) * 128, step * 128 : (step + 1) * 128] = here


def dot(left, right, contract):
    return lax.dot_general(left, right, (contract, ((), ())), preferred_element_type=jnp.float32)


def move(left, right, contract):
    high = left.astype(jnp.bfloat16)
    low = (left - high.astype(jnp.float32)).astype(jnp.bfloat16)
    return dot(high, right, contract) + dot(low, right, contract)


def edges_kernel(source, receiver, index, left, right, waves, places, sems):
    copies = [
        [
            pltpu.make_async_copy(field.at[part, wave], waves.at[kind, part, wave], sems.at[kind, 2 * part + wave])
            for part in range(2)
            for wave in range(2)
        ]
        for kind, field in enumerate((source, receiver))
    ]
    copies.append([pltpu.make_async_copy(index.at[depth], places.at[depth], sems.at[2, depth]) for depth in range(2)])
    for copy in sum(copies, []):
        copy.start()
    lane = lax.broadcasted_iota(jnp.int32, (ROWS, 128), 1)

    def join(parts, start):
        total = jnp.zeros((ROWS, 128), jnp.float32)
        for place, part in enumerate(parts):
            shift = (place * SIDE - start) % 128
            moved = part if shift == 0 else pltpu.roll(part, shift, 1)
            total = jnp.where((lane >= place * SIDE) & (lane < (place + 1) * SIDE), moved, total)
        return total

    ends = ((right, 1, 128 - SIDE), (left, 0, 0))
    for kind in range(3):
        for copy in copies[kind]:
            copy.wait()
        for out, tile, start in ends:
            cut = slice(tile * 128, (tile + 1) * 128)
            if kind < 2:
                out[kind] = join([waves[kind, part, wave, :, cut] for part in range(2) for wave in range(2)], start)
            else:
                out[2] = join([places[0, wave, :, cut].astype(jnp.float32) for wave in range(2)], start)


def own_kernel(waves, index, fields, indices, spread, joined):
    fill_spread(spread)
    matrix = spread[: 2 * COLS, :]
    for plane in range(6):
        for wave in range(2):
            cut = slice(wave * COLS, (wave + 1) * COLS)
            if plane < 4:
                joined[:, cut] = waves[plane // 2, plane % 2, wave]
            else:
                joined[:, cut] = index[plane - 4, wave].astype(jnp.float32)
        if plane < 4:
            values = move(joined[...], matrix, ((1,), (0,)))
        else:
            values = dot(joined[...].astype(jnp.bfloat16), matrix, ((1,), (0,)))
        for step in range(STEPS):
            piece = values[:, step * 128 : (step + 1) * 128]
            if plane < 4:
                fields[plane, step] = piece
            else:
                indices[plane - 4, step] = piece


def merge_kernel(own, indices, low, high, spread, fields, indices0, top, bottom, joined):
    lane = lax.broadcasted_iota(jnp.int32, (ROWS, 128), 1)
    matrix = spread[2 * COLS :, :]
    for plane in range(5):
        from_low, from_high = low[plane // 2], high[plane // 2]
        if plane % 2 == 0:
            from_high = pltpu.roll(from_high, 64, 1)
        else:
            from_low = pltpu.roll(from_low, 64, 1)
        joined[plane * ROWS : (plane + 1) * ROWS, :] = jnp.where(lane < 64, from_low, from_high)
    values = move(joined[...], matrix, ((1,), (0,)))
    for plane in range(5):
        for step in range(STEPS):
            piece = values[plane * ROWS : (plane + 1) * ROWS, step * 128 : (step + 1) * 128]
            if plane < 4:
                piece = piece + own[plane, step]
                fields[plane, step] = piece
                rows, at = HALO, (plane * STEPS + step) * HALO
            else:
                piece = piece + indices[0, step]
                indices0[step] = piece
                rows, at = INDEX_HALO, FIELD_ROWS + step * INDEX_HALO
            top[at : at + rows, :] = piece[:rows]
            bottom[at : at + rows, :] = piece[ROWS - rows :]


def advance(terms, past, plane, origin, ahead, count, mask, first):
    now = 0 if first else past + 1

    def rows(first_row):
        return pl.ds(first_row, 8, stride=count)

    def load(r):
        return [terms[now, plane, step, rows(origin + ahead + r), :] for step in range(STEPS)]

    values = [load(r) for r in range(-1, count + 1)]
    pairs = [[a + b for a, b in zip(values[r], values[r + 1])] for r in range(count + 1)]
    for r in range(count):
        column = [a + b for a, b in zip(pairs[r], pairs[r + 1])]
        from_left = pltpu.roll(column[STEPS - 1], 1, 1)
        from_right = pltpu.roll(column[0], 127, 1)
        across = [column[s] + column[s + 1] for s in range(STEPS - 1)]
        both = [(from_left + column[0]) + across[0]]
        both += [across[s - 1] + across[s] for s in range(1, STEPS - 1)]
        both.append(across[STEPS - 2] + (column[STEPS - 1] + from_right))
        for step in range(STEPS):
            moved = mask(step, r) * both[step]
            value = values[r + 1][step]
            if first:
                new = 0.5 * moved - value
            else:
                new = (moved - (value + value)) - terms[past, plane, step, rows(origin + 2 * ahead + r), :]
            terms[now + 1, plane, step, rows(origin + r), :] = new


def in_pairs(first, last, body):
    pairs = (last - first) // 2

    def two(at, carry):
        body(first + 2 * at, carry)
        return body(first + 2 * at + 1, carry)

    lax.fori_loop(0, pairs, two, 0)
    for at in range(first + 2 * pairs, last):
        body(at, 0)


def combine(terms, table, place, rows, step, orders):
    total = [None] * 4
    for order in range(orders):
        re = jnp.take_along_axis(jnp.broadcast_to(table[order, :][None], (8, 128)), place, axis=1)
        im = jnp.take_along_axis(jnp.broadcast_to(table[orders + order, :][None], (8, 128)), place, axis=1)
        for waves in (0, 2):
            real = terms[order, waves, step, rows(order), :]
            imag = terms[order, waves + 1, step, rows(order), :]
            if waves == 0:
                new = (re * real - im * imag, re * imag + im * real)
            else:
                new = (re * real + im * imag, re * imag - im * real)
            for part in range(2):
                old = total[waves + part]
                total[waves + part] = new[part] if old is None else old + new[part]
    return total


def fill(lookup, table):
    orders, parts, entries = table.shape
    lookup[...] = jnp.zeros(lookup.shape, jnp.float32)
    for order in range(orders):
        for part in range(parts):
            at = part * orders + order
            lookup[at : at + 1, :entries] = table[order, part : part + 1, :]


def column_mask(shape, step, flags):
    column = (lax.broadcasted_iota(jnp.int32, shape, 1) % 64) * STEPS + step
    return 0.25 * jnp.where(column < SIDE, flags[2:3, :], jnp.where(column >= SIDE + COLS, flags[3:4, :], 1.0))


def inner_kernel(
    flags, fields, indices0, indices1, table, strips0, strips1, picture, centre,
    terms, fresh, masks, places, lookup,
):
    orders = terms.shape[0]
    fill(lookup, table)
    for plane in range(4):
        for step in range(STEPS):
            terms[0, plane, step, :ROWS, :] = fields[plane, step]
    for step in range(STEPS):
        places[0, step] = indices0[step].astype(jnp.int32)
        places[1, step] = indices1[step].astype(jnp.int32)
        masks[step] = column_mask((8, 128), step, flags)

    def mask(step, r):
        return masks[step]

    for depth in range(2):
        height = ROWS - 2 * HALF * depth
        strips = (strips0, strips1)[depth]

        def hand_over(order, plane, strips=strips, height=height):
            for step in range(STEPS):
                strips[order, plane, step, :STRIP, :] = terms[order, plane, step, :STRIP, :]
                strips[order, plane, step, STRIP:, :] = terms[order, plane, step, pl.ds(height - STRIP - 2 * order, STRIP), :]

        for first, last in ((0, 1), (1, 3), (3, 7), (7, 11), (11, 12)):
            count = -(-(height - 2 * (first + 1)) // 8)
            count += count == 8

            def step_on(past, carry, first=first, count=count, hand_over=hand_over):
                for plane in range(4):
                    hand_over(0 if first == 0 else past + 1, plane)
                for plane in range(4):
                    advance(terms, past, plane, 0, 1, count, mask, first == 0)
                return carry

            start = max(first - 1, 0)
            if last - first == 1:
                step_on(start, 0)
            else:
                in_pairs(start, start + last - first, step_on)
        for plane in range(4):
            hand_over(orders - 1, plane)
        first_row = HALF * (depth + 1)
        count = (ROWS - 2 * first_row) // 8

        def gather(r, carry, depth=depth, first_row=first_row, count=count):
            own_rows = pl.ds(first_row + r, 8, stride=count)
            for step in range(STEPS):
                place = places[depth, step, own_rows, :]
                total = combine(terms, lookup, place, lambda k: pl.ds(HALF - k + r, 8, stride=count), step, orders)
                for plane in range(4):
                    fresh[plane, step, pl.ds(r, 8, stride=count), :] = total[plane]
                picture[depth, step, own_rows, :] = total[0] * total[2] + total[1] * total[3]
            return carry

        lax.fori_loop(0, count, gather, 0)
        for plane in range(4):
            for step in range(STEPS):
                piece = fresh[plane, step, : 8 * count, :]
                if depth == 0:
                    terms[0, plane, step, : 8 * count, :] = piece
                else:
                    centre[plane, step] = piece


def rim_kernel(
    flags, fields, indices0, indices1, above, below, strips0, strips1, inner_picture, table, spread, fresh, image,
    upper, lower, masks, places, picture, result, lookup,
):
    orders = upper.shape[0]
    fill(lookup, table)
    for plane in range(4):
        for step in range(STEPS):
            at = (plane * STEPS + step) * HALO
            upper[0, plane, step, :HALO, :] = above[at : at + HALO, :]
            upper[0, plane, step, HALO:, :] = fields[plane, step, :STRIP, :]
            lower[0, plane, step, :STRIP, :] = fields[plane, step, ROWS - STRIP :, :]
            lower[0, plane, step, STRIP:, :] = below[at : at + HALO, :]
    for step in range(STEPS):
        at = FIELD_ROWS + step * INDEX_HALO
        places[0, 0, step, :INDEX_HALO, :] = above[at : at + INDEX_HALO, :].astype(jnp.int32)
        places[0, 0, step, INDEX_HALO:, :] = indices0[step, :INDEX_HALO, :].astype(jnp.int32)
        places[0, 1, step, :INDEX_HALO, :] = indices0[step, ROWS - INDEX_HALO :, :].astype(jnp.int32)
        places[0, 1, step, INDEX_HALO:, :] = below[at : at + INDEX_HALO, :].astype(jnp.int32)
        places[1, 0, step] = indices1[step, : 2 * INDEX_HALO, :].astype(jnp.int32)
        places[1, 1, step] = indices1[step, ROWS - 2 * INDEX_HALO :, :].astype(jnp.int32)
        masks[step] = column_mask((8, 128), step, flags)
        for depth in range(2):
            picture[depth, step, OFFSET : OFFSET + ROWS, :] = inner_picture[depth, step]

    width = HALO // 8
    sublane = lax.broadcasted_iota(jnp.int32, (8, 128), 0) * width
    for depth in range(2):
        strips = (strips0, strips1)[depth]
        if depth == 1:
            for plane in range(4):
                for step in range(STEPS):
                    upper[0, plane, step, :HALO, :] = fresh[0, plane, step]
                    upper[0, plane, step, HALO:, :] = strips[0, plane, step, :STRIP, :]
                    lower[0, plane, step, :STRIP, :] = strips[0, plane, step, STRIP:, :]
                    lower[0, plane, step, STRIP:, :] = fresh[1, plane, step]

        def step_on(past, carry, first, depth=depth, strips=strips):
            order = 1 if first else past + 2
            shift = order - HALO + HALF * depth
            inside_upper = [jnp.where(sublane + (r + shift) >= 0, 1.0, flags[0:1, :]) for r in range(width)]
            inside_lower = [jnp.where(sublane + (r - HALO - shift) < 0, 1.0, flags[1:2, :]) for r in range(width)]
            for plane in range(4):
                for step in range(STEPS):
                    upper[order, plane, step, HALO:, :] = strips[order, plane, step, :STRIP, :]
                    lower[order, plane, step, :STRIP, :] = strips[order, plane, step, STRIP:, :]
            for plane in range(4):
                advance(upper, past, plane, 0, 1, width, lambda step, r: inside_upper[r] * masks[step], first)
            for plane in range(4):
                advance(lower, past, plane, STRIP, -1, width, lambda step, r: inside_lower[r] * masks[step], first)
            return carry

        step_on(0, 0, True)
        in_pairs(0, orders - 2, lambda past, carry: step_on(past, carry, False))

        def gather(r, carry, depth=depth):
            for side, terms in enumerate((upper, lower)):
                ahead, start = ((-1, HALF), (1, STRIP - HALF))[side]
                in_places = ((4, 4), (0, 8))[depth][side]
                in_picture = OFFSET + (-HALF + HALF * depth, ROWS - HALF - HALF * depth)[side]
                for step in range(STEPS):
                    place = places[depth, side, step, pl.ds(in_places + r, 8, stride=width), :]
                    total = combine(
                        terms, lookup, place, lambda k: pl.ds(start + ahead * k + r, 8, stride=width), step, orders
                    )
                    for plane in range(4):
                        fresh[side, plane, step, pl.ds(r, 8, stride=width), :] = total[plane]
                    picture[depth, step, pl.ds(in_picture + r, 8, stride=width), :] = total[0] * total[2] + total[1] * total[3]
            return carry

        lax.fori_loop(0, width, gather, 0)

    for step in range(STEPS):
        for depth in range(2):
            piece = picture[depth, step, OFFSET : OFFSET + ROWS, :]
            result[depth * ROWS : (depth + 1) * ROWS, step * 128 : (step + 1) * 128] = piece
    values = move(result[...], spread[: 2 * COLS, :], ((1,), (1,)))
    total = values[:, :COLS] + values[:, COLS:]
    for part in range(8):
        image[part] = total[part * BLOCK : (part + 1) * BLOCK]


def finish_kernel(fresh, centre, spread, source_out, receiver_out, result):
    for plane in range(4):
        for step in range(STEPS):
            rows, cut = plane * ROWS, slice(step * 128, (step + 1) * 128)
            result[rows : rows + HALO, cut] = fresh[0, plane, step]
            result[rows + HALO : rows + ROWS - HALO, cut] = centre[plane, step]
            result[rows + ROWS - HALO : rows + ROWS, cut] = fresh[1, plane, step]
    values = move(result[...], spread[: 2 * COLS, :], ((1,), (1,)))
    for plane in range(4):
        for wave in range(2):
            piece = values[plane * ROWS : (plane + 1) * ROWS, wave * COLS : (wave + 1) * COLS]
            (source_out, receiver_out)[plane // 2][plane % 2, wave] = piece


def full(count):
    return [pl.BlockSpec(memory_space=pltpu.VMEM)] * count


def shape(*dims, dtype=jnp.float32):
    return jax.ShapeDtypeStruct(dims, dtype)


def params(megabytes):
    return pltpu.CompilerParams(vmem_limit_bytes=megabytes * 1024 * 1024)


def cost(flops):
    return pl.CostEstimate(flops=flops, bytes_accessed=2**20, transcendentals=0)


def shift(block, axis, forward):
    count = lax.axis_size(axis)
    pairs = [(i, i + 1) for i in range(count - 1)]
    return lax.ppermute(block, axis, pairs if forward else [(b, a) for a, b in pairs])


def extrapolate(source, receiver, table_index, coef_table):
    orders = coef_table.shape[2]
    at_x, at_y = lax.axis_index("sx"), lax.axis_index("sy")
    row = lax.broadcasted_iota(jnp.int32, (8, 128), 0)
    flags = jnp.zeros((8, 128), jnp.float32)
    tests = [at_x > 0, at_x < lax.axis_size("sx") - 1, at_y > 0, at_y < lax.axis_size("sy") - 1]
    for place, test in enumerate(tests):
        flags = jnp.where((row == place) & test, 1.0, flags)
    table = jnp.transpose(coef_table, (2, 0, 1))

    left, right, waves, places = pl.pallas_call(
        edges_kernel,
        out_shape=(
            pltpu.VMEM((3, ROWS, 128), jnp.float32),
            pltpu.VMEM((3, ROWS, 128), jnp.float32),
            pltpu.VMEM((2, 2, 2, ROWS, COLS), jnp.float32),
            pltpu.VMEM((2, 2, ROWS, COLS), jnp.int32),
        ),
        in_specs=[pl.BlockSpec(memory_space=pltpu.HBM)] * 3,
        out_specs=tuple(full(4)),
        scratch_shapes=[pltpu.SemaphoreType.DMA((3, 4))],
        compiler_params=params(16),
        name="edges",
    )(*(pltpu.with_memory_space_constraint(array, pltpu.HBM) for array in (source, receiver, table_index)))
    low = shift(right, "sy", True)
    high = shift(left, "sy", False)
    own, indices, spread = pl.pallas_call(
        own_kernel,
        out_shape=(shape(4, STEPS, ROWS, 128), shape(2, STEPS, ROWS, 128), shape(WIDE, WIDE, dtype=jnp.bfloat16)),
        in_specs=full(2),
        out_specs=tuple(full(3)),
        scratch_shapes=[pltpu.VMEM((ROWS, 2 * COLS), jnp.float32)],
        compiler_params=params(16),
        cost_estimate=cost(2 * 10**9),
        name="own",
    )(waves, places)
    fields, indices0, top, bottom = pl.pallas_call(
        merge_kernel,
        out_shape=(shape(4, STEPS, ROWS, 128), shape(STEPS, ROWS, 128), shape(SEND, 128), shape(SEND, 128)),
        in_specs=full(5),
        out_specs=tuple(full(4)),
        scratch_shapes=[pltpu.VMEM((5 * ROWS, 128), jnp.float32)],
        compiler_params=params(16),
        name="merge",
    )(own, indices, low, high, spread)
    indices1 = indices[1]
    above = shift(bottom, "sx", True)
    below = shift(top, "sx", False)
    strip = shape(orders, 4, STEPS, 2 * STRIP, 128)
    lookup = pltpu.VMEM((2 * orders, 128), jnp.float32)
    strips0, strips1, picture, centre = pl.pallas_call(
        inner_kernel,
        out_shape=(strip, strip, shape(2, STEPS, ROWS, 128), shape(4, STEPS, ROWS - 2 * HALO, 128)),
        in_specs=full(5),
        out_specs=tuple(full(4)),
        scratch_shapes=[
            pltpu.VMEM((orders, 4, STEPS, ROWS + 16, 128), jnp.float32),
            pltpu.VMEM((4, STEPS, ROWS - HALO, 128), jnp.float32),
            pltpu.VMEM((STEPS, 8, 128), jnp.float32),
            pltpu.VMEM((2, STEPS, ROWS, 128), jnp.int32),
            lookup,
        ],
        compiler_params=params(32),
        cost_estimate=cost(10**10),
        name="inner",
    )(flags, fields, indices0, indices1, table)
    fresh, image = pl.pallas_call(
        rim_kernel,
        out_shape=(shape(2, 4, STEPS, HALO, 128), shape(8, BLOCK, COLS)),
        in_specs=full(11),
        out_specs=tuple(full(2)),
        scratch_shapes=[
            pltpu.VMEM((orders, 4, STEPS, HALO + STRIP, 128), jnp.float32),
            pltpu.VMEM((orders, 4, STEPS, HALO + STRIP, 128), jnp.float32),
            pltpu.VMEM((STEPS, 8, 128), jnp.float32),
            pltpu.VMEM((2, 2, STEPS, 2 * INDEX_HALO, 128), jnp.int32),
            pltpu.VMEM((2, STEPS, TALL, 128), jnp.float32),
            pltpu.VMEM((2 * ROWS, WIDE), jnp.float32),
            lookup,
        ],
        compiler_params=params(32),
        name="rim",
    )(flags, fields, indices0, indices1, above, below, strips0, strips1, picture, table, spread)
    source_out, receiver_out = pl.pallas_call(
        finish_kernel,
        out_shape=(shape(2, 2, ROWS, COLS), shape(2, 2, ROWS, COLS)),
        in_specs=full(3),
        out_specs=tuple(full(2)),
        scratch_shapes=[pltpu.VMEM((4 * ROWS, WIDE), jnp.float32)],
        compiler_params=params(16),
        cost_estimate=cost(2 * 10**9),
        name="finish",
    )(fresh, centre, spread)
    return source_out, receiver_out, image


def add_over_freq(pieces, beside):
    groups = [[y * 4 + z * 2 + core for y in range(4) for core in range(2)] for z in range(2)]
    mine = jnp.sum(lax.all_to_all(pieces, "freq", 0, 0, axis_index_groups=groups), axis=0)
    other = lax.ppermute(mine, "freq", [(i, i ^ 2) for i in range(16)])
    other, *beside = lax.optimization_barrier((other, *beside))
    mine = mine + other
    blocks = lax.all_to_all(jnp.broadcast_to(mine[None], pieces.shape), "freq", 0, 0, axis_index_groups=groups)
    return *beside, blocks.reshape(2, ROWS, COLS)


def local(source, receiver, table_index, coef_table):
    source_out, receiver_out, pieces = extrapolate(source, receiver, table_index, coef_table)
    return add_over_freq(pieces, (source_out, receiver_out))


def solution(mesh):
    placed = P(None, "freq", "sx", "sy")
    return jax.shard_map(
        local,
        mesh=mesh,
        in_specs=(placed, placed, placed, P()),
        out_specs=(placed, placed, P(None, "sx", "sy")),
        check_vma=False,
    )
```
